256 devices in a mesh: layer: 8 (over z_hi, y), tile: 32 (over x, z_lo, core).
Axes of the slice: x: 4, y: 4, z: 8 (z_hi: 2, z_lo: 4; z = z_hi * 4 + z_lo), core: 2. Of those that a mesh axis runs over, the one named last changes fastest.
Arguments:
- tau: bfloat16 [1024, 57600], P(None, ('layer', 'tile')), may hold values from -6 to 6
- vvvv: bfloat16 [128, 128, 57600], P('tile', None, 'layer'), may hold values from -0.0234375 to 0.0234375
- scales: float32 [128], P('tile'), may hold values from 0.5 to 2
- tile_ids: int32 [128], replicated, may hold values from 0 to 127, as said below
- counts: int32 [32], replicated, may hold values from 1 to 4, as said below
- spin_c: int32 [48], replicated, may hold values from 0 to 1
- spin_d: int32 [1200], replicated, may hold values from 0 to 1
- pair_energy: float32 [1024], P(('layer', 'tile')), may hold values from -1.5 to -0.5
- ab_energy: float32 [128, 128], replicated, may hold values from 1 to 3
Outputs:
- amplitudes: float32 [1024, 16384], P(('layer', 'tile'))
The draws below stay inside these ranges and needn't reach their ends.
Inputs may be any that keep to these rules, and one draw needn't show every extreme that they name: `tile_ids`: every ab tile appears exactly once; slot s of tile index t is entry t * 4 + s. The valid slots are the first counts[t] slots of tile index t; some index has all 4 valid.
All inputs are finite; a program needn't handle non-finite values.
Results may differ from the reference program's by a relative error of at most 0.0003.
Values may be sent and summed in bfloat16 or wider, within the bound.
A program may use at most 128 MiB of HBM per device.

```python
import math
import jax
import jax.numpy as jnp
from jax import lax

NV = 1200
CP = 48
TA = 128
SLOTS = 4
PAIRS = 1024
KDIM = 57600
NTILES = 128


def draw_tile_ids(key, part):
    key = jax.random.fold_in(key, 11)
    return jax.random.permutation(key, NTILES).astype(jnp.int32)


def draw_counts(key, part):
    key = jax.random.fold_in(key, 23)
    first, second = jax.random.split(key)
    owners = NTILES // SLOTS
    values = jax.random.randint(first, (owners,), 1, SLOTS + 1)
    chosen = jax.random.randint(second, (), 0, owners)
    values = jnp.where(jnp.arange(owners) == chosen, SLOTS, values)
    return values.astype(jnp.int32)


def with_ends(array, stream_key, least, high):
    shape = array.shape
    spot = [jax.random.randint(jax.random.fold_in(stream_key, axis), (), 0, shape[axis]) for axis in range(len(shape))]
    array = array.at[tuple(spot)].set(least)
    longest = shape.index(max(shape))
    spot[longest] = (spot[longest] + 1) % shape[longest]
    return array.at[tuple(spot)].set(high)


def levels(key, extent, cuts, least, high):
    gain, own = 1.0, jax.random.fold_in(key, 6)
    for axis_at, blocks in cuts:
        heights = jnp.exp(jax.random.uniform(jax.random.fold_in(own, axis_at), (blocks,), jnp.float32, least / len(cuts), high / len(cuts)))
        gain = gain * jnp.repeat(heights, extent[axis_at] // blocks).reshape([-1 if axis == axis_at else 1 for axis in range(len(extent))])
    return gain


def scatter_about(rng, extent, width, most, cuts=(), kind=jnp.bfloat16):
    factor_of = levels(rng, extent, cuts, -0.22, 0.18) if cuts else 1.0
    values = jax.random.normal(rng, extent, jnp.float32) * width * factor_of
    return jnp.minimum(jnp.maximum(values, -most), most).astype(kind)


def setup_inputs(seed: int = 0) -> dict:
    key_list = jax.random.split(jax.random.key(seed), 10)
    return {
        "tau": scatter_about(key_list[0], (PAIRS, KDIM), 1.0, 6.0, ((1, 256),)),
        "vvvv": scatter_about(key_list[1], (NTILES, TA, KDIM), KDIM ** -0.5, 0.0234375, ((0, 32), (2, 8))),
        "scales": jnp.clip(jnp.exp(math.log(2.0) - 1.3862944 * jax.random.uniform(key_list[2], (NTILES,), jnp.float32) ** levels(key_list[2], (NTILES,), ((0, 32),), -0.2, 0.2)), 0.5, 2.0),
        "tile_ids": draw_tile_ids(jax.random.fold_in(key_list[9], 71), 0),
        "counts": draw_counts(jax.random.fold_in(key_list[9], 71), 0),
        "spin_c": with_ends(jax.random.randint(key_list[5], (CP,), 0, 2), jax.random.fold_in(key_list[5], 1), 0, 1).astype(jnp.int32),
        "spin_d": with_ends(jax.random.randint(key_list[6], (NV,), 0, 2), jax.random.fold_in(key_list[6], 1), 0, 1).astype(jnp.int32),
        "pair_energy": jnp.clip(-1.5 + 1.0 * jax.random.uniform(key_list[7], (PAIRS,), jnp.float32) ** levels(key_list[7], (PAIRS,), ((0, 256),), -0.2, 0.2), -1.5, -0.5),
        "ab_energy": jnp.clip(jax.random.uniform(key_list[8], (NTILES, TA), jnp.float32, 1.0, 3.0), 1.0, 3.0),
    }


def reference(tau, vvvv, scales, tile_ids, counts, spin_c, spin_d, pair_energy, ab_energy):
    weight = jnp.where(spin_c[:, None] == spin_d[None, :], 0.5, 1.0).reshape(KDIM)
    tau_weighted = tau * weight.astype(jnp.bfloat16)[None, :]

    def one_slot(stored):
        return lax.dot_general(tau_weighted, stored, (((1,), (1,)), ((), ())), preferred_element_type=jnp.float32)

    partial_value = lax.map(one_slot, vvvv) * scales[:, None, None]
    slot_index = jnp.arange(NTILES, dtype=jnp.int32)
    owner = slot_index // SLOTS
    valid = (slot_index % SLOTS) < counts[owner]
    onehot = ((tile_ids[:, None] == slot_index[None, :]) & valid[:, None]).astype(jnp.float32)
    residual = jnp.einsum("gpa,gj->pja", partial_value, onehot, precision=lax.Precision.HIGHEST)
    denom = ab_energy[None, :, :] - pair_energy[:, None, None]
    return (residual / denom).reshape(PAIRS, NTILES * TA)
```

```python
import functools

import jax
import jax.numpy as jnp
from jax import lax
from jax.experimental import pallas as pl
from jax.experimental.pallas import tpu as pltpu
from jax.sharding import PartitionSpec as P

MESH = pl.DeviceIdType.MESH

NX, NZ, NK, NY, NH = 4, 4, 2, 4, 2
LANES = 128
CHUNKS = 8
ROWS = 240
PAD = 256
A_ROWS = 192


def ladder_kernel(
    tau_ref,
    v_hbm,
    scales_ref,
    spin_c_ref,
    spin_d_ref,
    out_ref,
    t_buf,
    v_buf,
    vt_buf,
    w_buf,
    acc,
    r_buf,
    y_buf,
    q_buf,
    z_buf,
    s_buf,
    v_sem,
    az_s,
    az_r,
    ax_s,
    ax_r,
    bx_s,
    bx_r,
    bz_s,
    bz_r,
    sa_s,
    sa_r,
    sb_s,
    sb_r,
    y_s,
    y_r,
    z_s,
    z_r,
    x_s,
    x_r,
):
    layer = lax.axis_index("layer")
    tile = lax.axis_index("tile")
    xx, zz, kk = tile // 8, (tile // 2) % 4, tile % 2
    hh, yy = layer // 4, layer % 4
    kpiece = tau_ref.shape[0]
    klayer = v_hbm.shape[1]
    virtual = spin_d_ref.shape[1]
    panel = spin_c_ref.shape[1]

    def xdev(x):
        return (layer, x * 8 + zz * 2 + kk)

    def zdev(z):
        return (layer, xx * 8 + z * 2 + kk)

    sib = (layer, xx * 8 + zz * 2 + (1 - kk))

    def ydev(y):
        return (hh * 4 + y, tile)

    def ring(h, z, k):
        return (h * 4 + yy, xx * 8 + z * 2 + k)

    barrier = pltpu.get_barrier_semaphore()

    def greet(dev):
        pl.semaphore_signal(barrier, inc=1, device_id=dev, device_id_type=MESH)

    for step in range(1, NX):
        greet(xdev((xx + step) % NX))
    for step in range(1, NY):
        greet(ydev((yy + step) % NY))
    greet(sib)
    for step in range(1, NH * NZ):
        place = (hh * NZ + zz + step) % (NH * NZ)
        for core in range(NK):
            greet(ring(place // NZ, place % NZ, core))

    v_copy = pltpu.make_async_copy(v_hbm, v_buf.at[:, pl.ds(0, klayer)], v_sem)
    v_copy.start()
    v_buf[:, klayer:, :] = jnp.zeros((v_buf.shape[0], v_buf.shape[1] - klayer, 128), v_buf.dtype)

    start = (kpiece * tile) // 16 * 16
    offset = kpiece * tile - start
    base = layer * klayer + start
    c_first = base // virtual
    d_first = base - c_first * virtual
    row = lax.broadcasted_iota(jnp.int32, (ROWS, 1), 0)
    d_index = row + d_first
    over = d_index >= virtual
    d_index = jnp.where(over, d_index - virtual, d_index)
    c_index = jnp.where(over, c_first + 1, c_first)
    d_iota = lax.broadcasted_iota(jnp.int32, (ROWS, virtual), 1)
    c_iota = lax.broadcasted_iota(jnp.int32, (ROWS, panel), 1)
    spin_right = jnp.sum(jnp.where(d_iota == d_index, spin_d_ref[...], 0).astype(jnp.float32), axis=1, keepdims=True)
    spin_left = jnp.sum(jnp.where(c_iota == c_index, spin_c_ref[...], 0).astype(jnp.float32), axis=1, keepdims=True)
    factor = jnp.where(spin_left == spin_right, 0.5, 1.0)
    shift = (
        lax.broadcasted_iota(jnp.int32, (ROWS, kpiece), 0) - offset
        == lax.broadcasted_iota(jnp.int32, (ROWS, kpiece), 1)
    )
    placed = jnp.dot(
        shift.astype(jnp.float32).astype(jnp.bfloat16), tau_ref[...], preferred_element_type=jnp.float32
    )
    w_buf[...] = (placed * factor).astype(jnp.bfloat16)

    def clear(step, carry):
        t_buf[step // 32, step // 8 % 4, step // 2 % 4, step % 2, ROWS:, :] = jnp.zeros((PAD - ROWS, LANES), jnp.bfloat16)
        return carry

    lax.fori_loop(0, CHUNKS * NX * NZ * NK, clear, 0)

    pl.semaphore_wait(barrier, (NX - 1) + (NY - 1) + 1 + (NH * NZ - 1) * NK)

    part_a = pl.ds(0, A_ROWS)
    part_b = pl.ds(A_ROWS, ROWS - A_ROWS)

    def copy(src, dst, ssem, rsem, dev):
        return pltpu.make_async_remote_copy(
            src_ref=src, dst_ref=dst, send_sem=ssem, recv_sem=rsem, device_id=dev, device_id_type=MESH
        )

    def same(ref, ssem, rsem, dev):
        return copy(ref, ref, ssem, rsem, dev)

    def up(c, z0):
        return same(t_buf.at[c, xx, z0, kk, part_a], az_s.at[c, z0, 0], az_r.at[c, z0], zdev(zz + 1))

    def down(c, z0):
        return same(t_buf.at[c, xx, z0, kk, part_a], az_s.at[c, z0, 1], az_r.at[c, z0], zdev(zz - 1))

    def b_up(c, z0):
        return same(t_buf.at[c, :, z0, kk, part_b], bz_s.at[c, z0, 0], bz_r.at[c, z0], zdev(zz + 1))

    def b_down(c, z0):
        return same(t_buf.at[c, :, z0, kk, part_b], bz_s.at[c, z0, 1], bz_r.at[c, z0], zdev(zz - 1))

    def turn(c, z0):
        return 1 - 2 * ((c + z0) % 2)

    def ax(c, z0, way):
        if way == 2:
            s = turn(c, z0)
            return same(
                t_buf.at[c, (xx - s + 4) % 4, z0, kk, part_a], ax_s.at[c, z0, 2], ax_r.at[c, z0, 2], xdev((xx + s + 4) % 4)
            )
        s = 1 - 2 * way
        return same(t_buf.at[c, xx, z0, kk, part_a], ax_s.at[c, z0, way], ax_r.at[c, z0, way], xdev((xx + s + 4) % 4))

    def ax_in(c, z0, way):
        source = (xx + (3, 1, 2)[way]) % 4
        return same(t_buf.at[c, source, z0, kk, part_a], ax_s.at[c, z0, way], ax_r.at[c, z0, way], xdev(source))

    def bx(c, way):
        if way == 2:
            s = turn(c, 0)
            return same(t_buf.at[c, (xx - s + 4) % 4, zz, kk, part_b], bx_s.at[c, 2], bx_r.at[c, 2], xdev((xx + s + 4) % 4))
        s = 1 - 2 * way
        return same(t_buf.at[c, xx, zz, kk, part_b], bx_s.at[c, way], bx_r.at[c, way], xdev((xx + s + 4) % 4))

    def bx_in(c, way):
        source = (xx + (3, 1, 2)[way]) % 4
        return same(t_buf.at[c, source, zz, kk, part_b], bx_s.at[c, way], bx_r.at[c, way], xdev(source))

    def sa(c, z0, core):
        return same(t_buf.at[c, :, z0, core, part_a], sa_s.at[c, z0], sa_r.at[c, z0], sib)

    def sb(c, z0, core):
        return same(t_buf.at[c, :, z0, core, part_b], sb_s.at[c, z0], sb_r.at[c, z0], sib)

    def sides(distance, act):
        for sign in (-1, 1):
            z0 = zz + sign * distance

            @pl.when((z0 >= 0) & (z0 < NZ))
            def _():
                act(z0, sign)

    def pass_on(z0, sign, send_up, send_down):
        def go(fn, edge):
            @pl.when(edge)
            def _():
                fn()

        if sign <= 0:
            go(send_up, zz < NZ - 1)
        if sign >= 0:
            go(send_down, zz > 0)

    def z_step(c, distance):
        def act(z0, sign):
            up(c, z0).wait_recv()
            pass_on(z0, sign, lambda: up(c, z0).start(), lambda: down(c, z0).start())
            ax(c, z0, 0).start()
            ax(c, z0, 1).start()

        sides(distance, act)

    def far_step(c, distance):
        def act(z0, sign):
            ax_in(c, z0, 0).wait_recv()
            ax_in(c, z0, 1).wait_recv()
            ax(c, z0, 2).start()

        act(zz, 0) if distance == 0 else sides(distance, act)

    def row_step(c, distance):
        def act(z0, sign):
            ax_in(c, z0, 2).wait_recv()
            sa(c, z0, kk).start()

        act(zz, 0) if distance == 0 else sides(distance, act)

    def b_step(c, distance):
        def act(z0, sign):
            if distance == 0:
                bx_in(c, 2).wait_recv()
            else:
                b_up(c, z0).wait_recv()
            pass_on(z0, sign, lambda: b_up(c, z0).start(), lambda: b_down(c, z0).start())
            sb(c, z0, kk).start()

        act(zz, 0) if distance == 0 else sides(distance, act)

    def own_step(c):
        q = lax.broadcasted_iota(jnp.int32, (1, LANES), 1)
        q_y, q_h, q_z, q_x = q // 32, q // 16 % 2, q // 4 % 4, q % 4
        pair = (q_h * 4 + q_y) * 128 + (q_x * 8 + q_z * 2 + c % 2) * 4 + c // 2
        pick = lax.broadcasted_iota(jnp.int32, (tau_ref.shape[1], LANES), 0) == pair
        block = jnp.dot(
            w_buf[...], pick.astype(jnp.float32).astype(jnp.bfloat16), preferred_element_type=jnp.float32
        )
        t_buf[c, xx, zz, kk, 0:ROWS, :] = block.astype(jnp.bfloat16)
        pass_on(zz, 0, lambda: up(c, zz).start(), lambda: down(c, zz).start())
        bx(c, 0).start()
        bx(c, 1).start()
        ax(c, zz, 0).start()
        ax(c, zz, 1).start()

    def bx_step(c):
        bx_in(c, 0).wait_recv()
        bx_in(c, 1).wait_recv()
        bx(c, 2).start()

    def turn_v(step):
        def one(i, carry):
            t = step * 8 + i
            first = pl.multiple_of((kpiece * t) // 16 * 16, 16)
            lanes = pl.ds(pl.multiple_of(t * PAD, PAD), PAD)
            for s in range(v_buf.shape[0]):
                vt_buf[s * 128 : (s + 1) * 128, lanes] = v_buf[s, pl.ds(first, PAD), :].T
            return carry

        lax.fori_loop(0, 8, one, 0)

    def sib_wait(c):
        def one(z0, carry):
            sa(c, z0, 1 - kk).wait_recv()
            sb(c, z0, 1 - kk).wait_recv()
            return carry

        lax.fori_loop(0, NZ, one, 0)

    def multiply(c, x):
        block = t_buf[c, x].reshape(NZ * NK * PAD, LANES)
        product = jnp.dot(
            vt_buf[:, x * NZ * NK * PAD : (x + 1) * NZ * NK * PAD], block, preferred_element_type=jnp.float32
        )
        if x == 0:
            acc[...] = product
        else:
            acc[...] += product

    def y_out(c, step):
        other = (yy + step) % NY
        rows = pl.ds(pl.multiple_of(other * 32, 32), 32)
        return copy(r_buf.at[c, rows], y_buf.at[c, 3 - step], y_s.at[c, step - 1], y_r.at[c, 3 - step], ydev(other))

    def y_in(c, slot):
        return copy(y_buf.at[c, slot], y_buf.at[c, slot], y_s.at[c, slot], y_r.at[c, slot], ydev((yy + slot + 1) % NY))

    def y_step(c):
        for s in range(v_buf.shape[0]):
            r_buf[c, :, s * 128 : (s + 1) * 128] = (acc[s * 128 : (s + 1) * 128, :] * scales_ref[s]).T
        for step in (2, 1, 3):
            y_out(c, step).start()

    def z_out(c, place):
        return copy(
            q_buf.at[c, place],
            z_buf.at[c // 2, (hh * NZ + zz) * NK + kk],
            z_s.at[c, place],
            z_r.at[c // 2, (hh * NZ + zz) * NK + kk],
            ring(place // NZ, place % NZ, c % 2),
        )

    def z_in(j, source):
        return copy(z_buf.at[j, source], z_buf.at[j, source], z_s.at[0, 0], z_r.at[j, source], sib)

    def zs_step(c):
        for slot in range(3):
            y_in(c, slot).wait_recv()
        mine = r_buf[c, pl.ds(pl.multiple_of(yy * 32, 32), 32), :]
        total = mine + y_buf[c, 0] + y_buf[c, 1] + y_buf[c, 2]
        for place in range(NH * NZ):
            q_buf[c, place] = total[place * 4 : place * 4 + 4, :]

        @pl.when(kk == c % 2)
        def _():
            z_buf[c // 2, (hh * NZ + zz) * NK + kk] = q_buf[c, hh * NZ + zz]

        @pl.when(kk != c % 2)
        def _():
            z_out(c, hh * NZ + zz).start()

        def one(step, carry):
            z_out(c, (hh * NZ + zz + step) % (NH * NZ)).start()
            return carry

        lax.fori_loop(1, NH * NZ, one, 0)

    def x_out(j, step):
        other = (xx + step) % NX
        return copy(s_buf.at[j, other], out_ref.at[j, xx], x_s.at[j, step - 1], x_r.at[j, 3 - step], xdev(other))

    def x_in(j, slot):
        source = (xx + slot + 1) % NX
        return copy(out_ref.at[j, source], out_ref.at[j, source], x_s.at[j, slot], x_r.at[j, slot], xdev(source))

    def xs_step(c):
        j = c // 2

        @pl.when(kk == c % 2)
        def _():
            def one(source, carry):
                @pl.when(source != (hh * NZ + zz) * NK + kk)
                def _():
                    z_in(j, source).wait_recv()

                return carry

            lax.fori_loop(0, NH * NZ * NK, one, 0)
            for source in range(NZ * NK):
                both = z_buf[j, source] + z_buf[j, NZ * NK + source]
                for x in range(NX):
                    s_buf[j, x, source : source + 1, :] = both[x : x + 1, :]
            for step in (2, 1, 3):
                x_out(j, step).start()
            out_ref[j, xx] = s_buf[j, xx]

    def when_in(c, act):
        @pl.when((c >= 0) & (c < CHUNKS))
        def _():
            act()

    own_step(0)

    def tick(tau, carry):
        when_in(tau + 1, lambda: own_step(tau + 1))
        when_in(tau - 8, lambda: xs_step(tau - 8))
        when_in(tau - 7, lambda: zs_step(tau - 7))
        c = tau - 6

        when_in(c, lambda: sib_wait(c))
        when_in(tau - 5, lambda: (b_step(tau - 5, 3), row_step(tau - 5, 3)))
        when_in(c, lambda: multiply(c, 0))
        when_in(tau - 4, lambda: (b_step(tau - 4, 2), row_step(tau - 4, 2), far_step(tau - 4, 3)))
        when_in(c, lambda: multiply(c, 1))
        when_in(
            tau - 3,
            lambda: (b_step(tau - 3, 1), row_step(tau - 3, 1), far_step(tau - 3, 2), z_step(tau - 3, 3)),
        )
        when_in(c, lambda: multiply(c, 2))
        when_in(
            tau - 2,
            lambda: (b_step(tau - 2, 0), row_step(tau - 2, 0), far_step(tau - 2, 1), z_step(tau - 2, 2)),
        )
        when_in(c, lambda: multiply(c, 3))
        when_in(tau - 1, lambda: (bx_step(tau - 1), z_step(tau - 1, 1), far_step(tau - 1, 0)))
        when_in(c, lambda: y_step(c))

        @pl.when(tau == 0)
        def _():
            v_copy.wait()

        @pl.when(tau < 4)
        def _():
            turn_v(tau)

        return carry

    lax.fori_loop(0, CHUNKS + 8, tick, 0)

    def last(c, carry):
        j = c // 2

        @pl.when(kk == c % 2)
        def _():
            for slot in range(3):
                x_in(j, slot).wait_recv()
            for step in range(1, NX):
                x_out(j, step).wait_send()

        @pl.when(kk != c % 2)
        def _():
            z_out(c, hh * NZ + zz).wait_send()

        def one(step, carry):
            z_out(c, (hh * NZ + zz + step) % (NH * NZ)).wait_send()
            return carry

        lax.fori_loop(1, NH * NZ, one, 0)
        for step in range(1, NY):
            y_out(c, step).wait_send()
        for way in range(3):
            bx(c, way).wait_send()

        def rows(z0, carry):
            for way in range(3):
                ax(c, z0, way).wait_send()
            sa(c, z0, kk).wait_send()
            sb(c, z0, kk).wait_send()

            @pl.when((z0 <= zz) & (zz < NZ - 1))
            def _():
                up(c, z0).wait_send()
                b_up(c, z0).wait_send()

            @pl.when((z0 >= zz) & (zz > 0))
            def _():
                down(c, z0).wait_send()
                b_down(c, z0).wait_send()

            return carry

        lax.fori_loop(0, NZ, rows, 0)
        return carry

    lax.fori_loop(0, CHUNKS, last, 0)


def local(tau, vvvv, scales, tile_ids, counts, spin_c, spin_d, pair_energy, ab_energy):
    slots, width, klayer = vvvv.shape
    pairs, kpiece = tau.shape
    ntile = lax.axis_size("tile")
    nlayer = lax.axis_size("layer")
    own_pairs = pairs // (nlayer * ntile)
    all_slots = slots * ntile
    vmem = pl.BlockSpec(memory_space=pltpu.VMEM)
    bf16, f32 = jnp.bfloat16, jnp.float32
    dma = pltpu.SemaphoreType.DMA
    owned = pl.pallas_call(
        ladder_kernel,
        out_shape=jax.ShapeDtypeStruct((own_pairs, NX, NZ * NK, slots * width), f32),
        in_specs=[vmem, pl.BlockSpec(memory_space=pl.ANY), pl.BlockSpec(memory_space=pltpu.SMEM), vmem, vmem],
        out_specs=vmem,
        scratch_shapes=[
            pltpu.VMEM((CHUNKS, NX, NZ, NK, PAD, LANES), bf16),
            pltpu.VMEM((slots, klayer + 16, width), bf16),
            pltpu.VMEM((slots * width, ntile * PAD), bf16),
            pltpu.VMEM((ROWS, pairs), bf16),
            pltpu.VMEM((slots * width, LANES), f32),
            pltpu.VMEM((CHUNKS, LANES, slots * width), f32),
            pltpu.VMEM((CHUNKS, NY - 1, LANES // NY, slots * width), f32),
            pltpu.VMEM((CHUNKS, NH * NZ, NX, slots * width), f32),
            pltpu.VMEM((own_pairs, NH * NZ * NK, NX, slots * width), f32),
            pltpu.VMEM((own_pairs, NX, NZ * NK, slots * width), f32),
            dma,
            dma((CHUNKS, NZ, 2)),
            dma((CHUNKS, NZ)),
            dma((CHUNKS, NZ, 3)),
            dma((CHUNKS, NZ, 3)),
            dma((CHUNKS, 3)),
            dma((CHUNKS, 3)),
            dma((CHUNKS, NZ, 2)),
            dma((CHUNKS, NZ)),
            dma((CHUNKS, NZ)),
            dma((CHUNKS, NZ)),
            dma((CHUNKS, NZ)),
            dma((CHUNKS, NZ)),
            dma((CHUNKS, 3)),
            dma((CHUNKS, 3)),
            dma((CHUNKS, NH * NZ)),
            dma((own_pairs, NH * NZ * NK)),
            dma((own_pairs, 3)),
            dma((own_pairs, 3)),
        ],
        compiler_params=pltpu.CompilerParams(
            collective_id=0, has_side_effects=True, vmem_limit_bytes=56 * 1024 * 1024
        ),
        name="ladder",
    )(tau.T, jnp.swapaxes(vvvv, 1, 2), scales, spin_c[None, :], spin_d[None, :])
    slot_index = jnp.arange(all_slots, dtype=jnp.int32)
    owner = slot_index // slots
    owner_count = jnp.sum(
        jnp.where(owner[:, None] == jnp.arange(ntile, dtype=jnp.int32)[None, :], counts[None, :], 0), axis=1
    )
    valid = slot_index % slots < owner_count
    onehot = ((tile_ids[:, None] == slot_index[None, :]) & valid[:, None]).astype(jnp.float32)
    residual = jnp.einsum(
        "pga,gj->pja",
        owned.reshape(own_pairs, all_slots, width),
        onehot,
        precision=lax.Precision.HIGHEST,
    )
    denom = ab_energy[None, :, :] - pair_energy[:, None, None]
    return (residual / denom).reshape(own_pairs, all_slots * width)


def solution(mesh):
    placed = (
        P(None, ("layer", "tile")),
        P("tile", None, "layer"),
        P("tile"),
        P(),
        P(),
        P(),
        P(),
        P(("layer", "tile")),
        P(),
    )
    return jax.shard_map(
        local, mesh=mesh, in_specs=placed, out_specs=P(("layer", "tile"), None), check_vma=False
    )
```

```python
import functools

import jax
import jax.numpy as jnp
from jax import lax
from jax.experimental import pallas as pl
from jax.experimental.pallas import tpu as pltpu
from jax.sharding import PartitionSpec as P

MESH = pl.DeviceIdType.MESH

NX, NZ, NK, NY, NH = 4, 4, 2, 4, 2
LANES = 128
CHUNKS = 8
ROWS = 240
PAD = 256
A_ROWS = 192


def ladder_kernel(
    tau_ref,
    v_hbm,
    scales_ref,
    spin_c_ref,
    spin_d_ref,
    out_ref,
    t_buf,
    v_buf,
    vt_buf,
    w_buf,
    acc,
    r_buf,
    y_buf,
    q_buf,
    z_buf,
    s_buf,
    v_sem,
    send_sem,
    az_r,
    ax_r,
    bx_r,
    bz_r,
    sib_r,
    y_r,
    z_r,
    x_r,
):
    layer = lax.axis_index("layer")
    tile = lax.axis_index("tile")
    xx, zz, kk = tile // 8, (tile // 2) % 4, tile % 2
    hh, yy = layer // 4, layer % 4
    kpiece = tau_ref.shape[0]
    klayer = v_hbm.shape[1]
    virtual = spin_d_ref.shape[1]
    panel = spin_c_ref.shape[1]

    def xdev(x):
        return (layer, x * 8 + zz * 2 + kk)

    def zdev(z):
        return (layer, xx * 8 + z * 2 + kk)

    sib = (layer, xx * 8 + zz * 2 + (1 - kk))

    def ydev(y):
        return (hh * 4 + y, tile)

    def ring(h, z, k):
        return (h * 4 + yy, xx * 8 + z * 2 + k)

    barrier = pltpu.get_barrier_semaphore()

    def greet(dev):
        pl.semaphore_signal(barrier, inc=1, device_id=dev, device_id_type=MESH)

    for step in range(1, NX):
        greet(xdev((xx + step) % NX))
    for step in range(1, NY):
        greet(ydev((yy + step) % NY))
    greet(sib)
    for step in range(1, NH * NZ):
        place = (hh * NZ + zz + step) % (NH * NZ)
        for core in range(NK):
            greet(ring(place // NZ, place % NZ, core))

    v_copy = pltpu.make_async_copy(v_hbm, v_buf.at[:, pl.ds(0, klayer)], v_sem)
    v_copy.start()
    v_buf[:, klayer:, :] = jnp.zeros((v_buf.shape[0], v_buf.shape[1] - klayer, 128), v_buf.dtype)

    start = (kpiece * tile) // 16 * 16
    offset = kpiece * tile - start
    base = layer * klayer + start
    c_first = base // virtual
    d_first = base - c_first * virtual
    row = lax.broadcasted_iota(jnp.int32, (ROWS, 1), 0)
    d_index = row + d_first
    over = d_index >= virtual
    d_index = jnp.where(over, d_index - virtual, d_index)
    c_index = jnp.where(over, c_first + 1, c_first)
    d_iota = lax.broadcasted_iota(jnp.int32, (ROWS, virtual), 1)
    c_iota = lax.broadcasted_iota(jnp.int32, (ROWS, panel), 1)
    spin_right = jnp.sum(jnp.where(d_iota == d_index, spin_d_ref[...], 0).astype(jnp.float32), axis=1, keepdims=True)
    spin_left = jnp.sum(jnp.where(c_iota == c_index, spin_c_ref[...], 0).astype(jnp.float32), axis=1, keepdims=True)
    factor = jnp.where(spin_left == spin_right, 0.5, 1.0)
    shift = (
        lax.broadcasted_iota(jnp.int32, (ROWS, kpiece), 0) - offset
        == lax.broadcasted_iota(jnp.int32, (ROWS, kpiece), 1)
    )
    placed = jnp.dot(
        shift.astype(jnp.float32).astype(jnp.bfloat16), tau_ref[...], preferred_element_type=jnp.float32
    )
    w_buf[...] = (placed * factor).astype(jnp.bfloat16)

    def clear(step, carry):
        t_buf[step // 32, step // 8 % 4, step // 2 % 4, step % 2, ROWS:, :] = jnp.zeros((PAD - ROWS, LANES), jnp.bfloat16)
        return carry

    lax.fori_loop(0, CHUNKS * NX * NZ * NK, clear, 0)

    part_a = pl.ds(0, A_ROWS)
    part_b = pl.ds(A_ROWS, ROWS - A_ROWS)

    def copy(src, dst, ssem, rsem, dev):
        return pltpu.make_async_remote_copy(
            src_ref=src, dst_ref=dst, send_sem=ssem, recv_sem=rsem, device_id=dev, device_id_type=MESH
        )

    def same(ref, ssem, rsem, dev):
        return copy(ref, ref, ssem, rsem, dev)

    az_s, ax_s, bx_s, bz_s, sib_s, y_s, z_s, zk_s, x_s = (send_sem.at[i] for i in range(9))

    def az(c, z0, way):
        return same(t_buf.at[c, xx, z0, kk, part_a], az_s, az_r.at[c, z0], zdev(zz + way))

    def bz(c, z0, way):
        return same(t_buf.at[c, :, z0, kk, part_b], bz_s, bz_r.at[c, z0], zdev(zz + way))

    def turn(c, z0):
        return 1 - 2 * ((c + z0) % 2)

    def ax(c, z0, way):
        s = turn(c, z0) if way == 2 else 1 - 2 * way
        source = (xx - s + 4) % 4 if way == 2 else xx
        return same(t_buf.at[c, source, z0, kk, part_a], ax_s, ax_r.at[c, z0, way // 2], xdev((xx + s + 4) % 4))

    def ax_near(c, z0):
        return same(t_buf.at[c, 0:2, z0, kk, part_a], ax_s, ax_r.at[c, z0, 0], sib)

    def ax_far(c, z0):
        return same(t_buf.at[c, (xx + 2) % 4, z0, kk, part_a], ax_s, ax_r.at[c, z0, 1], sib)

    def bx(c, way):
        s = turn(c, 0) if way == 2 else 1 - 2 * way
        source = (xx - s + 4) % 4 if way == 2 else xx
        return same(t_buf.at[c, source, zz, kk, part_b], bx_s, bx_r.at[c, way // 2], xdev((xx + s + 4) % 4))

    def bx_near(c):
        return same(t_buf.at[c, 0:2, zz, kk, part_b], bx_s, bx_r.at[c, 0], sib)

    def bx_far(c):
        return same(t_buf.at[c, (xx + 2) % 4, zz, kk, part_b], bx_s, bx_r.at[c, 1], sib)

    def sb(c, z0):
        return same(t_buf.at[c, :, z0, kk, 0:ROWS], sib_s, sib_r.at[c], sib)

    def sides(distance, act):
        for sign in (-1, 1):
            z0 = zz + sign * distance

            @pl.when((z0 >= 0) & (z0 < NZ))
            def _():
                act(z0, sign)

    def pass_on(sign, send):
        if sign <= 0:

            @pl.when(zz < NZ - 1)
            def _():
                send(1)

        if sign >= 0:

            @pl.when(zz > 0)
            def _():
                send(-1)

    def z_step(c, distance):
        def act(z0, sign):
            az(c, z0, 0).wait_recv()
            pass_on(sign, lambda way: az(c, z0, way).start())
            ax(c, z0, 0).start()
            ax(c, z0, 1).start()

        sides(distance, act)

    def far_step(c, distance):
        def act(z0, sign):
            ax_near(c, z0).wait_recv()
            ax(c, z0, 2).start()

        act(zz, 0) if distance == 0 else sides(distance, act)

    def row_step(c, distance):
        def act(z0, sign):
            if distance == 0:
                bx_far(c).wait_recv()
            else:
                bz(c, z0, 0).wait_recv()
            pass_on(sign, lambda way: bz(c, z0, way).start())
            ax_far(c, z0).wait_recv()
            sb(c, z0).start()

        act(zz, 0) if distance == 0 else sides(distance, act)

    def own_fill(c):
        q = lax.broadcasted_iota(jnp.int32, (1, LANES), 1)
        q_y, q_h, q_z, q_x = q // 32, q // 16 % 2, q // 4 % 4, q % 4
        pair = (q_h * 4 + q_y) * 128 + (q_x * 8 + q_z * 2 + c % 2) * 4 + c // 2
        pick = lax.broadcasted_iota(jnp.int32, (tau_ref.shape[1], LANES), 0) == pair
        block = jnp.dot(
            w_buf[...], pick.astype(jnp.float32).astype(jnp.bfloat16), preferred_element_type=jnp.float32
        )
        t_buf[c, xx, zz, kk, 0:ROWS, :] = block.astype(jnp.bfloat16)

    def own_send(c):
        pass_on(0, lambda way: az(c, zz, way).start())
        bx(c, 0).start()
        bx(c, 1).start()
        ax(c, zz, 0).start()
        ax(c, zz, 1).start()

    def bx_step(c):
        bx_near(c).wait_recv()
        bx(c, 2).start()

    def turn_v(step):
        def one(i, carry):
            t = step * 8 + i
            first = pl.multiple_of((kpiece * t) // 16 * 16, 16)
            lanes = pl.ds(pl.multiple_of(t * PAD, PAD), PAD)
            for s in range(v_buf.shape[0]):
                vt_buf[s * 128 : (s + 1) * 128, lanes] = v_buf[s, pl.ds(first, PAD), :].T
            return carry

        lax.fori_loop(0, 8, one, 0)

    def multiply(c, x):
        block = t_buf[c, x].reshape(NZ * NK * PAD, LANES)
        product = jnp.dot(
            vt_buf[:, x * NZ * NK * PAD : (x + 1) * NZ * NK * PAD], block, preferred_element_type=jnp.float32
        )
        if x == 0:
            acc[...] = product
        else:
            acc[...] += product

    def y_out(c, step):
        other = (yy + step) % NY
        rows = pl.ds(pl.multiple_of(other * 32, 32), 32)
        return copy(r_buf.at[c, rows], y_buf.at[c, 3 - step], y_s, y_r.at[c], ydev(other))

    def y_step(c):
        for s in range(v_buf.shape[0]):
            r_buf[c, :, s * 128 : (s + 1) * 128] = (acc[s * 128 : (s + 1) * 128, :] * scales_ref[s]).T
        for step in (2, 1, 3):
            y_out(c, step).start()

    def z_out(c, place, sem):
        mine = (hh * NZ + zz) * NK + kk
        return copy(
            q_buf.at[c, place], z_buf.at[c // 2, mine], sem, z_r.at[c // 2], ring(place // NZ, place % NZ, c % 2)
        )

    def zs_step(c):
        same(y_buf.at[c], y_s, y_r.at[c], sib).wait_recv()
        mine = r_buf[c, pl.ds(pl.multiple_of(yy * 32, 32), 32), :]
        total = mine + y_buf[c, 0] + y_buf[c, 1] + y_buf[c, 2]
        for place in range(NH * NZ):
            q_buf[c, place] = total[place * 4 : place * 4 + 4, :]

        @pl.when(kk == c % 2)
        def _():
            z_buf[c // 2, (hh * NZ + zz) * NK + kk] = q_buf[c, hh * NZ + zz]

        @pl.when(kk != c % 2)
        def _():
            z_out(c, hh * NZ + zz, zk_s).start()

        def one(step, carry):
            z_out(c, (hh * NZ + zz + step) % (NH * NZ), z_s).start()
            return carry

        lax.fori_loop(1, NH * NZ, one, 0)

    def x_out(j, step):
        other = (xx + step) % NX
        return copy(s_buf.at[j, other], out_ref.at[j, xx], x_s, x_r, xdev(other))

    def xs_step(c):
        j = c // 2

        @pl.when(kk == c % 2)
        def _():
            received = z_buf.at[j, 0 : NH * NZ * NK - 1]
            same(received, z_s, z_r.at[j], sib).wait_recv()
            for source in range(NZ * NK):
                both = z_buf[j, source] + z_buf[j, NZ * NK + source]
                for x in range(NX):
                    s_buf[j, x, source : source + 1, :] = both[x : x + 1, :]
            for step in (2, 1, 3):
                x_out(j, step).start()
            out_ref[j, xx] = s_buf[j, xx]

    def when_in(c, act):
        @pl.when((c >= 0) & (c < CHUNKS))
        def _():
            act()

    own_fill(0)
    own_fill(1)
    pl.semaphore_wait(barrier, (NX - 1) + (NY - 1) + 1 + (NH * NZ - 1) * NK)
    own_send(0)

    def tick(tau, carry):
        when_in(tau + 1, lambda: own_send(tau + 1))
        c = tau - 6
        when_in(c, lambda: same(t_buf.at[c, :, :, 1 - kk, 0:ROWS], sib_s, sib_r.at[c], sib).wait_recv())
        when_in(tau - 1, lambda: (bx_step(tau - 1), z_step(tau - 1, 1), far_step(tau - 1, 0)))
        when_in(c, lambda: multiply(c, 0))
        when_in(tau - 2, lambda: (row_step(tau - 2, 0), far_step(tau - 2, 1), z_step(tau - 2, 2)))
        when_in(c, lambda: multiply(c, 1))
        when_in(tau - 3, lambda: (row_step(tau - 3, 1), far_step(tau - 3, 2), z_step(tau - 3, 3)))
        when_in(c, lambda: multiply(c, 2))
        when_in(tau - 4, lambda: (row_step(tau - 4, 2), far_step(tau - 4, 3)))
        when_in(c, lambda: multiply(c, 3))
        when_in(tau - 5, lambda: row_step(tau - 5, 3))
        when_in(c, lambda: y_step(c))
        when_in(tau - 7, lambda: zs_step(tau - 7))
        when_in(tau - 8, lambda: xs_step(tau - 8))

        @pl.when(tau == 0)
        def _():
            v_copy.wait()

        @pl.when(tau < 4)
        def _():
            turn_v(tau)

        when_in(tau + 2, lambda: own_fill(tau + 2))
        return carry

    lax.fori_loop(0, CHUNKS + 8, tick, 0)

    def sent(ref, sem):
        same(ref, sem, sem, sib).wait_send()

    sent(t_buf.at[:, 0:3, :, 0, part_a], ax_s)
    sent(t_buf.at[:, 0:3, 0, 0, part_b], bx_s)
    sent(t_buf.at[:, :, :, 0, 0:ROWS], sib_s)

    @pl.when((zz == 0) | (zz == NZ - 1))
    def _():
        sent(t_buf.at[:, 0, 0, 0, part_a], az_s)
        sent(t_buf.at[:, :, 0, 0, part_b], bz_s)

    @pl.when((zz > 0) & (zz < NZ - 1))
    def _():
        sent(t_buf.at[0:5, 0:2, :, 0, part_a], az_s)
        sent(t_buf.at[0:5, :, :, :, part_b], bz_s)

    sent(r_buf.at[:, 0:96], y_s)
    sent(q_buf.at[:, 0 : NH * NZ - 1], z_s)
    sent(q_buf.at[0 : CHUNKS // 2, 0], zk_s)
    sent(s_buf.at[:, 0 : NX - 1], x_s)
    same(out_ref.at[:, 0 : NX - 1], x_s, x_r, sib).wait_recv()


def local(tau, vvvv, scales, tile_ids, counts, spin_c, spin_d, pair_energy, ab_energy):
    slots, width, klayer = vvvv.shape
    pairs, kpiece = tau.shape
    ntile = lax.axis_size("tile")
    nlayer = lax.axis_size("layer")
    own_pairs = pairs // (nlayer * ntile)
    all_slots = slots * ntile
    vmem = pl.BlockSpec(memory_space=pltpu.VMEM)
    bf16, f32 = jnp.bfloat16, jnp.float32
    dma = pltpu.SemaphoreType.DMA
    owned = pl.pallas_call(
        ladder_kernel,
        out_shape=jax.ShapeDtypeStruct((own_pairs, NX, NZ * NK, slots * width), f32),
        in_specs=[vmem, pl.BlockSpec(memory_space=pl.ANY), pl.BlockSpec(memory_space=pltpu.SMEM), vmem, vmem],
        out_specs=vmem,
        scratch_shapes=[
            pltpu.VMEM((CHUNKS, NX, NZ, NK, PAD, LANES), bf16),
            pltpu.VMEM((slots, klayer + 16, width), bf16),
            pltpu.VMEM((slots * width, ntile * PAD), bf16),
            pltpu.VMEM((ROWS, pairs), bf16),
            pltpu.VMEM((slots * width, LANES), f32),
            pltpu.VMEM((CHUNKS, LANES, slots * width), f32),
            pltpu.VMEM((CHUNKS, NY - 1, LANES // NY, slots * width), f32),
            pltpu.VMEM((CHUNKS, NH * NZ, NX, slots * width), f32),
            pltpu.VMEM((own_pairs, NH * NZ * NK, NX, slots * width), f32),
            pltpu.VMEM((own_pairs, NX, NZ * NK, slots * width), f32),
            dma,
            dma((9,)),
            dma((CHUNKS, NZ)),
            dma((CHUNKS, NZ, 2)),
            dma((CHUNKS, 2)),
            dma((CHUNKS, NZ)),
            dma((CHUNKS,)),
            dma((CHUNKS,)),
            dma((own_pairs,)),
            dma,
        ],
        compiler_params=pltpu.CompilerParams(
            collective_id=0, has_side_effects=True, vmem_limit_bytes=56 * 1024 * 1024
        ),
        name="ladder",
    )(tau.T, jnp.swapaxes(vvvv, 1, 2), scales, spin_c[None, :], spin_d[None, :])
    slot_index = jnp.arange(all_slots, dtype=jnp.int32)
    owner = slot_index // slots
    owner_count = jnp.sum(
        jnp.where(owner[:, None] == jnp.arange(ntile, dtype=jnp.int32)[None, :], counts[None, :], 0), axis=1
    )
    valid = slot_index % slots < owner_count
    onehot = ((tile_ids[:, None] == slot_index[None, :]) & valid[:, None]).astype(jnp.float32)
    residual = jnp.einsum(
        "pga,gj->pja",
        owned.reshape(own_pairs, all_slots, width),
        onehot,
        precision=lax.Precision.HIGHEST,
    )
    denom = ab_energy[None, :, :] - pair_energy[:, None, None]
    return (residual / denom).reshape(own_pairs, all_slots * width)


def solution(mesh):
    placed = (
        P(None, ("layer", "tile")),
        P("tile", None, "layer"),
        P("tile"),
        P(),
        P(),
        P(),
        P(),
        P(("layer", "tile")),
        P(),
    )
    return jax.shard_map(
        local, mesh=mesh, in_specs=placed, out_specs=P(("layer", "tile"), None), check_vma=False
    )
```

```python
import functools

import jax
import jax.numpy as jnp
from jax import lax
from jax.experimental import pallas as pl
from jax.experimental.pallas import tpu as pltpu
from jax.sharding import PartitionSpec as P

MESH = pl.DeviceIdType.MESH

NX, NZ, NK, NY, NH = 4, 4, 2, 4, 2
UNITS = ((3, (0,)), (0, (0, 1)), (1, (0, 1)), (2, (0, 1)), (3, (1,)))
LANES = tuple(128 * len(cores) for _, cores in UNITS)
COUNT = len(UNITS)
ROWS = 240
PAD = 256
A_ROWS = 176


def ladder_kernel(
    tau_ref,
    v_hbm,
    scales_ref,
    spin_c_ref,
    spin_d_ref,
    ids_ref,
    counts_ref,
    pair_ref,
    ab_ref,
    out_ref,
    own_buf,
    pick_buf,
    t_bufs,
    v_buf,
    vt_buf,
    w_buf,
    accs,
    r_bufs,
    y_bufs,
    q_bufs,
    z_bufs,
    s_buf,
    v_sem,
    send_sem,
    x_s,
    az_r,
    ax_r,
    bx_r,
    bz_r,
    sib_r,
    y_r,
    z_r,
    x_r,
):
    layer = lax.axis_index("layer")
    tile = lax.axis_index("tile")
    xx, zz, kk = tile // 8, (tile // 2) % 4, tile % 2
    hh, yy = layer // 4, layer % 4
    kpiece = tau_ref.shape[0]
    klayer = v_hbm.shape[1]
    virtual = spin_d_ref.shape[0]
    panel = spin_c_ref.shape[0]

    place = hh * NZ + zz

    def xdev(x, core=None):
        return (layer, x * 8 + zz * 2 + (kk if core is None else core))

    def zdev(z):
        return (layer, xx * 8 + z * 2 + kk)

    sib = xdev(xx, 1 - kk)

    def ydev(y):
        return (hh * 4 + y, tile)

    def ring(other):
        return (other // NZ * 4 + yy, xx * 8 + other % NZ * 2 + kk)

    barrier = pltpu.get_barrier_semaphore()

    def greet(dev):
        pl.semaphore_signal(barrier, inc=1, device_id=dev, device_id_type=MESH)

    for step in range(1, NH * NZ):
        greet(ring((place + step) % (NH * NZ)))
    for step in range(1, NX):
        greet(xdev((xx + step) % NX))
    for step in range(1, NY):
        greet(ydev((yy + step) % NY))
    for step in range(NX):
        greet(xdev((xx + step) % NX, 1 - kk))

    v_copy = pltpu.make_async_copy(v_hbm, v_buf.at[:, pl.ds(0, klayer)], v_sem)
    v_copy.start()
    v_buf[:, klayer:, :] = jnp.zeros((v_buf.shape[0], v_buf.shape[1] - klayer, 128), v_buf.dtype)

    start = (kpiece * tile) // 16 * 16
    offset = kpiece * tile - start
    base = layer * klayer + start
    c_first = base // virtual
    d_first = base - c_first * virtual
    row = lax.broadcasted_iota(jnp.int32, (ROWS, 1), 0)
    d_index = row + d_first
    over = d_index >= virtual
    d_index = jnp.where(over, d_index - virtual, d_index)
    c_index = jnp.where(over, c_first + 1, c_first)
    d_iota = lax.broadcasted_iota(jnp.int32, (ROWS, virtual), 1)
    c_iota = lax.broadcasted_iota(jnp.int32, (ROWS, panel), 1)
    spin_right = jnp.sum(jnp.where(d_iota == d_index, spin_d_ref[...][None, :], 0).astype(jnp.float32), axis=1, keepdims=True)
    spin_left = jnp.sum(jnp.where(c_iota == c_index, spin_c_ref[...][None, :], 0).astype(jnp.float32), axis=1, keepdims=True)
    factor = jnp.where(spin_left == spin_right, 0.5, 1.0)
    shift = (
        lax.broadcasted_iota(jnp.int32, (ROWS, kpiece), 0) - offset
        == lax.broadcasted_iota(jnp.int32, (ROWS, kpiece), 1)
    )
    placed = jnp.dot(
        shift.astype(jnp.float32).astype(jnp.bfloat16), tau_ref[...], preferred_element_type=jnp.float32
    )
    w_buf[...] = (placed * factor).astype(jnp.bfloat16)

    def clear(step, carry):
        for t_buf in t_bufs:
            t_buf[step // 8, step // 2 % 4, step % 2, ROWS:, :] = jnp.zeros((PAD - ROWS, t_buf.shape[-1]), jnp.bfloat16)
        return carry

    lax.fori_loop(0, NX * NZ * NK, clear, 0)

    part_a = pl.ds(0, A_ROWS)
    part_b = pl.ds(A_ROWS, ROWS - A_ROWS)

    def copy(src, dst, ssem, rsem, dev):
        return pltpu.make_async_remote_copy(
            src_ref=src, dst_ref=dst, send_sem=ssem, recv_sem=rsem, device_id=dev, device_id_type=MESH
        )

    def same(ref, ssem, rsem, dev):
        return copy(ref, ref, ssem, rsem, dev)

    def kind(u, i):
        return send_sem.at[u, i]

    def az(u, z0, way):
        return same(t_bufs[u].at[z0, xx, kk, part_a], kind(u, 0 if way > 0 else 7), az_r.at[u, z0], zdev(zz + way))

    def bz(u, z0, way):
        return same(t_bufs[u].at[z0, :, kk, part_b], kind(u, 1 if way > 0 else 8), bz_r.at[u, z0], zdev(zz + way))

    def turn(u, z0):
        return 1 - 2 * ((u + z0) % 2)

    def ax(u, z0, way):
        s = turn(u, z0) if way == 2 else 1 - 2 * way
        source = (xx - s + 4) % 4 if way == 2 else xx
        return same(t_bufs[u].at[z0, source, kk, part_a], kind(u, 2), ax_r.at[u, z0, way // 2], xdev((xx + s + 4) % 4))

    def ax_near(u, z0):
        return same(t_bufs[u].at[z0, 0:2, kk, part_a], kind(u, 2), ax_r.at[u, z0, 0], sib)

    def ax_far(u, z0):
        return same(t_bufs[u].at[z0, (xx + 2) % 4, kk, part_a], kind(u, 2), ax_r.at[u, z0, 1], sib)

    def bx(u, way):
        s = turn(u, 0) if way == 2 else 1 - 2 * way
        source = (xx - s + 4) % 4 if way == 2 else xx
        return same(t_bufs[u].at[zz, source, kk, part_b], kind(u, 3), bx_r.at[u, way // 2], xdev((xx + s + 4) % 4))

    def bx_near(u):
        return same(t_bufs[u].at[zz, 0:2, kk, part_b], kind(u, 3), bx_r.at[u, 0], sib)

    def bx_far(u):
        return same(t_bufs[u].at[zz, (xx + 2) % 4, kk, part_b], kind(u, 3), bx_r.at[u, 1], sib)

    def sb(u, z0):
        return same(t_bufs[u].at[z0, :, kk, 0:ROWS], kind(u, 4), sib_r.at[u, z0], sib)

    def sides(distance, act):
        for sign in (-1, 1):
            z0 = zz + sign * distance

            @pl.when((z0 >= 0) & (z0 < NZ))
            def _():
                act(z0, sign)

    def pass_on(sign, send):
        if sign <= 0:

            @pl.when(zz < NZ - 1)
            def _():
                send(1)

        if sign >= 0:

            @pl.when(zz > 0)
            def _():
                send(-1)

    def rows_at(distance, act):
        act(zz, 0) if distance == 0 else sides(distance, act)

    def z_step(u, distance):
        def act(z0, sign):
            az(u, z0, 0).wait_recv()
            pass_on(sign, lambda way: az(u, z0, way).start())
            ax(u, z0, 0).start()
            ax(u, z0, 1).start()

        sides(distance, act)

    def far_step(u, distance):
        def act(z0, sign):
            ax_near(u, z0).wait_recv()
            ax(u, z0, 2).start()

        rows_at(distance, act)

    def row_step(u, distance):
        def act(z0, sign):
            if distance == 0:
                bx_far(u).wait_recv()
            else:
                bz(u, z0, 0).wait_recv()
            pass_on(sign, lambda way: bz(u, z0, way).start())
            ax_far(u, z0).wait_recv()
            sb(u, z0).start()

        rows_at(distance, act)

    def own_fill(u):
        j, cores = UNITS[u]
        n, lanes = len(cores), LANES[u]
        q = lax.broadcasted_iota(jnp.int32, (1, lanes), 1)
        q_y, q_h, q_z, q_k, q_x = q // (32 * n), q // (16 * n) % 2, q // (4 * n) % 4, q // 4 % n + cores[0], q % 4
        pair = (q_h * 4 + q_y) * 128 + (q_x * 8 + q_z * 2 + q_k) * 4 + j
        pick = lax.broadcasted_iota(jnp.int32, (tau_ref.shape[1], lanes), 0) == pair
        block = jnp.dot(
            w_buf[...], pick.astype(jnp.float32).astype(jnp.bfloat16), preferred_element_type=jnp.float32
        )
        t_bufs[u][zz, xx, kk, 0:ROWS, :] = block.astype(jnp.bfloat16)

    def own_send(u):
        pass_on(0, lambda way: az(u, zz, way).start())
        bx(u, 0).start()
        bx(u, 1).start()
        ax(u, zz, 0).start()
        ax(u, zz, 1).start()

    def bx_step(u):
        bx_near(u).wait_recv()
        bx(u, 2).start()

    def turn_v(step):
        def one(i, carry):
            t = step * 16 + i
            first = pl.multiple_of((kpiece * t) // 16 * 16, 16)
            block = (t // 2 % NZ * NX + t // 8) * NK + t % NK
            lanes = pl.ds(pl.multiple_of(block * PAD, PAD), PAD)
            for s in range(v_buf.shape[0]):
                vt_buf[s * 128 : (s + 1) * 128, lanes] = v_buf[s, pl.ds(first, PAD), :].T
            return carry

        lax.fori_loop(0, 16, one, 0)

    def multiply(u, distance):
        depth = NX * NK * PAD

        def act(z0, sign):
            t_bufs_row = t_bufs[u].at[z0]
            same(t_bufs_row.at[:, 1 - kk, 0:ROWS], kind(u, 4), sib_r.at[u, z0], sib).wait_recv()
            if distance == 0:
                accs[u][...] = jnp.zeros(accs[u].shape, jnp.float32)

            def one(i, carry):
                size = depth // 2
                part = vt_buf[:, pl.ds(pl.multiple_of(z0 * depth + i * size, size), size)]
                block = t_bufs_row[pl.ds(i * 2, 2)].reshape(size, LANES[u])
                accs[u][...] += jnp.dot(part, block, preferred_element_type=jnp.float32)
                return carry

            lax.fori_loop(0, 2, one, 0)

        rows_at(distance, act)

    def y_step(u):
        r_buf = r_bufs[u]
        quarter = r_buf.shape[0] // NY
        for half in range(LANES[u] // 128):
            lanes = slice(half * 128, half * 128 + 128)
            for s in range(v_buf.shape[0]):
                rows = slice(s * 128, s * 128 + 128)
                r_buf[lanes, rows] = (accs[u][rows, lanes] * scales_ref[s]).T
        for step in (2, 1, 3):
            other = (yy + step) % NY
            rows = pl.ds(pl.multiple_of(other * quarter, quarter), quarter)
            copy(r_buf.at[rows], y_bufs[u].at[3 - step], kind(u, 5), y_r.at[u], ydev(other)).start()

    def zs_step(u):
        r_buf, y_buf, q_buf, z_buf = r_bufs[u], y_bufs[u], q_bufs[u], z_bufs[u]
        quarter = r_buf.shape[0] // NY
        rows = q_buf.shape[1]
        same(y_buf, kind(u, 5), y_r.at[u], sib).wait_recv()
        mine = r_buf[pl.ds(pl.multiple_of(yy * quarter, quarter), quarter), :]
        total = mine + y_buf[0] + y_buf[1] + y_buf[2]
        for other in range(NH * NZ):
            q_buf[other] = total[other * rows : (other + 1) * rows, :]
        z_buf[place] = q_buf[place]
        for step in (4, 3, 5, 2, 6, 1, 7):
            other = (place + step) % (NH * NZ)
            copy(q_buf.at[other], z_buf.at[place], kind(u, 6), z_r.at[u], ring(other)).start()

    def xs_step(u):
        z_buf = z_bufs[u]
        j, cores = UNITS[u]
        same(z_buf.at[0 : NH * NZ - 1], kind(u, 6), z_r.at[u], sib).wait_recv()
        for z in range(NZ):
            both = z_buf[z] + z_buf[NZ + z]
            for i, core in enumerate(cores):
                for x in range(NX):
                    s_buf[j, core * NX + x, z : z + 1, :] = both[i * NX + x : i * NX + x + 1, :]

        def send(core, step):
            other = (xx + step) % NX
            copy(s_buf.at[j, core * NX + other], own_buf.at[j, xx * NK + kk], x_s, x_r, xdev(other, core)).start()

        for core in cores:

            @pl.when(kk == core)
            def _():
                for step in (2, 1, 3):
                    send(core, step)
                own_buf[j, xx * NK + kk] = s_buf[j, core * NX + xx]

            @pl.when(kk != core)
            def _():
                for step in (2, 1, 3, 0):
                    send(core, step)

    def sent(ref, sem):
        same(ref, sem, sem, sib).wait_send()

    def gather_sent(u):
        t_buf = t_bufs[u]
        sent(t_buf.at[0:3, :, 0, part_a], kind(u, 2))
        sent(t_buf.at[0:3, 0, 0, part_b], kind(u, 3))
        sent(t_buf.at[:, :, 0, 0:ROWS], kind(u, 4))

        for v in range(NZ):

            @pl.when(zz == v)
            def _():
                for count, i in ((v + 1 if v < NZ - 1 else 0, 0), (NZ - v if v > 0 else 0, 7)):
                    if count:
                        sent(t_buf.at[0, 0:count, 0, part_a], kind(u, i))
                        sent(t_buf.at[:, 0:count, 0, part_b], kind(u, i + 1))

    def slot_pick():
        slots, owners = v_buf.shape[0], NX * NK * NZ
        g = lax.broadcasted_iota(jnp.int32, (owners, slots * owners), 1)
        t = lax.broadcasted_iota(jnp.int32, (owners, slots * owners), 0)
        held = jnp.where(g // slots == t, 1.0, 0.0).astype(jnp.bfloat16)
        counts = jnp.broadcast_to(counts_ref[...][None, :], (8, owners)).astype(jnp.float32).astype(jnp.bfloat16)
        count = jnp.dot(counts, held, preferred_element_type=jnp.float32)
        ids = jnp.broadcast_to(ids_ref[...][None, :], count.shape).astype(jnp.float32)
        slot = lax.broadcasted_iota(jnp.int32, count.shape, 1) % slots
        ids = jnp.where(slot.astype(jnp.float32) < count, ids, -1.0).astype(jnp.bfloat16)
        g = lax.broadcasted_iota(jnp.int32, (slots * owners, owners), 0)
        r = lax.broadcasted_iota(jnp.int32, (slots * owners, owners), 1)
        t = r // (NK * NZ) * (NK * NZ) + r % NZ * NK + r // NZ % NK
        j = lax.broadcasted_iota(jnp.int32, (slots * owners, owners), 0).astype(jnp.float32)
        for s in range(slots):
            order = jnp.where(g == t * slots + s, 1.0, 0.0).astype(jnp.bfloat16)
            mine = jnp.dot(ids, order, preferred_element_type=jnp.float32)
            pick_buf[s] = jnp.where(mine[0:1, :] == j, 1.0, 0.0)

    own_fill(0)
    own_fill(1)
    slot_pick()
    pl.semaphore_wait(barrier, (NX - 1) + (NY - 1) + (NH * NZ - 1) + NX)
    own_send(0)

    for tick in range(COUNT + 8):

        def at(stage, act):
            if 0 <= tick - stage < COUNT:
                act(tick - stage)

        at(-1, own_send)
        at(1, lambda u: (bx_step(u), z_step(u, 1), far_step(u, 0)))
        at(3, lambda u: multiply(u, 0))
        at(2, lambda u: (row_step(u, 0), far_step(u, 1), z_step(u, 2)))
        at(4, lambda u: multiply(u, 1))
        at(3, lambda u: (row_step(u, 1), far_step(u, 2), z_step(u, 3)))
        at(5, lambda u: multiply(u, 2))
        at(4, lambda u: (row_step(u, 2), far_step(u, 3)))
        at(5, lambda u: row_step(u, 3))
        at(6, lambda u: multiply(u, 3))
        at(6, y_step)
        at(7, zs_step)
        at(8, xs_step)
        if tick == 0:
            v_copy.wait()
        if tick < 2:
            turn_v(tick)
        at(-2, own_fill)
        at(6, gather_sent)

    for u in range(COUNT):
        sent(r_bufs[u].at[0 : r_bufs[u].shape[0] // 4 * 3], kind(u, 5))
        sent(q_bufs[u].at[0 : NH * NZ - 1], kind(u, 6))
    sent(s_buf.at[:, 0 : NX * NK - 1], x_s)
    same(own_buf.at[:, 0 : NX * NK - 1], x_s, x_r, sib).wait_recv()
    width = ab_ref.shape[1]
    for p in range(own_buf.shape[0]):
        owned = own_buf[p].reshape(NX * NK * NZ, own_buf.shape[3])
        residual = jnp.zeros(ab_ref.shape, jnp.float32)
        for s in range(v_buf.shape[0]):
            residual += jnp.dot(
                pick_buf[s],
                owned[:, s * width : (s + 1) * width],
                precision=lax.Precision.HIGHEST,
                preferred_element_type=jnp.float32,
            )
        out_ref[:, p, :] = residual / (ab_ref[...] - pair_ref[p])


def local(tau, vvvv, scales, tile_ids, counts, spin_c, spin_d, pair_energy, ab_energy):
    slots, width, klayer = vvvv.shape
    pairs, kpiece = tau.shape
    ntile = lax.axis_size("tile")
    nlayer = lax.axis_size("layer")
    own_pairs = pairs // (nlayer * ntile)
    all_slots = slots * ntile
    vmem = pl.BlockSpec(memory_space=pltpu.VMEM)
    bf16, f32 = jnp.bfloat16, jnp.float32
    dma = pltpu.SemaphoreType.DMA
    columns = slots * width
    smem = pl.BlockSpec(memory_space=pltpu.SMEM)
    amplitudes = pl.pallas_call(
        ladder_kernel,
        out_shape=jax.ShapeDtypeStruct((all_slots, own_pairs, width), f32),
        in_specs=[vmem, pl.BlockSpec(memory_space=pl.ANY), smem, vmem, vmem, vmem, vmem, smem, vmem],
        out_specs=vmem,
        scratch_shapes=[
            pltpu.VMEM((own_pairs, NX * NK, NZ, columns), f32),
            pltpu.VMEM((slots, all_slots, ntile), f32),
            [pltpu.VMEM((NZ, NX, NK, PAD, lanes), bf16) for lanes in LANES],
            pltpu.VMEM((slots, klayer + 16, width), bf16),
            pltpu.VMEM((columns, ntile * PAD), bf16),
            pltpu.VMEM((ROWS, pairs), bf16),
            [pltpu.VMEM((columns, lanes), f32) for lanes in LANES],
            [pltpu.VMEM((lanes, columns), f32) for lanes in LANES],
            [pltpu.VMEM((NY - 1, lanes // NY, columns), f32) for lanes in LANES],
            [pltpu.VMEM((NH * NZ, lanes // 32, columns), f32) for lanes in LANES],
            [pltpu.VMEM((NH * NZ, lanes // 32, columns), f32) for lanes in LANES],
            pltpu.VMEM((own_pairs, NX * NK, NZ, columns), f32),
            dma,
            dma((COUNT, 9)),
            dma,
            dma((COUNT, NZ)),
            dma((COUNT, NZ, 2)),
            dma((COUNT, 2)),
            dma((COUNT, NZ)),
            dma((COUNT, NZ)),
            dma((COUNT,)),
            dma((COUNT,)),
            dma,
        ],
        compiler_params=pltpu.CompilerParams(
            collective_id=0, has_side_effects=True, vmem_limit_bytes=56 * 1024 * 1024
        ),
        name="ladder",
    )(tau.T, jnp.swapaxes(vvvv, 1, 2), scales, spin_c, spin_d, tile_ids, counts, pair_energy, ab_energy)
    return jnp.swapaxes(amplitudes, 0, 1).reshape(own_pairs, all_slots * width)


def solution(mesh):
    placed = (
        P(None, ("layer", "tile")),
        P("tile", None, "layer"),
        P("tile"),
        P(),
        P(),
        P(),
        P(),
        P(("layer", "tile")),
        P(),
    )
    return jax.shard_map(
        local, mesh=mesh, in_specs=placed, out_specs=P(("layer", "tile"), None), check_vma=False
    )
```

```python
import functools

import jax
import jax.numpy as jnp
from jax import lax
from jax.experimental import pallas as pl
from jax.experimental.pallas import tpu as pltpu
from jax.sharding import PartitionSpec as P

MESH = pl.DeviceIdType.MESH

NX, NZ, NK, NY, NH = 4, 4, 2, 4, 2
UNITS = ((3, (0,)), (0, (0, 1)), (1, (0, 1)), (2, (0, 1)), (3, (1,)))
LANES = tuple(128 * len(cores) for _, cores in UNITS)
COUNT = len(UNITS)
LAST = COUNT - 1
ROWS = 240
FEW = 224
PAD = 256
A_ROWS = 176


def ladder_kernel(
    tau_ref,
    v_hbm,
    scales_ref,
    spin_c_ref,
    spin_d_ref,
    ids_ref,
    counts_ref,
    pair_ref,
    ab_ref,
    out_ref,
    own_buf,
    pick_buf,
    t_bufs,
    v_buf,
    vt_buf,
    w_buf,
    edge_buf,
    accs,
    r_bufs,
    y_bufs,
    q_bufs,
    z_bufs,
    s_buf,
    v_sem,
    edge_sem,
    send_sem,
    az_r,
    ax_r,
    bx_r,
    bz_r,
    sib_r,
    y_r,
    z_r,
    x_r,
):
    layer = lax.axis_index("layer")
    tile = lax.axis_index("tile")
    xx, zz, kk = tile // 8, (tile // 2) % 4, tile % 2
    hh, yy = layer // 4, layer % 4
    kpiece = tau_ref.shape[0]
    klayer = v_hbm.shape[1]
    virtual = spin_d_ref.shape[0]
    panel = spin_c_ref.shape[0]

    place = hh * NZ + zz

    def xdev(x, core=None):
        return (layer, x * 8 + zz * 2 + (kk if core is None else core))

    def zdev(z):
        return (layer, xx * 8 + z * 2 + kk)

    sib = xdev(xx, 1 - kk)

    def ydev(y):
        return (hh * 4 + y, tile)

    def ring(other, core=None):
        return (other // NZ * 4 + yy, xx * 8 + other % NZ * 2 + (kk if core is None else core))

    def plane(y, x):
        return (hh * 4 + y, x * 8 + zz * 2 + kk)

    barrier = pltpu.get_barrier_semaphore()

    def greet(dev):
        pl.semaphore_signal(barrier, inc=1, device_id=dev, device_id_type=MESH)

    for step in range(1, NH * NZ):
        for core in range(NK):
            greet(ring((place + step) % (NH * NZ), core))
    for step in range(1, NY):
        for turn in range(NX):
            greet(plane((yy + step) % NY, (xx + turn) % NX))
    for step in range(1, NX):
        greet(xdev((xx + step) % NX))
    for step in range(NX):
        greet(xdev((xx + step) % NX, 1 - kk))
    tiles = NX * NZ * NK
    greet((layer, (tile + 1) % tiles))
    greet((layer, (tile + tiles - 1) % tiles))

    v_copy = pltpu.make_async_copy(v_hbm, v_buf.at[:, pl.ds(0, klayer)], v_sem)
    v_copy.start()
    v_buf[:, klayer:, :] = jnp.zeros((v_buf.shape[0], v_buf.shape[1] - klayer, 128), v_buf.dtype)

    start = (kpiece * tile) // 16 * 16
    offset = kpiece * tile - start
    base = layer * klayer + start
    c_first = base // virtual
    d_first = base - c_first * virtual
    row = lax.broadcasted_iota(jnp.int32, (ROWS, 1), 0)
    d_index = row + d_first
    over = d_index >= virtual
    d_index = jnp.where(over, d_index - virtual, d_index)
    c_index = jnp.where(over, c_first + 1, c_first)
    d_iota = lax.broadcasted_iota(jnp.int32, (ROWS, virtual), 1)
    c_iota = lax.broadcasted_iota(jnp.int32, (ROWS, panel), 1)
    spin_right = jnp.sum(jnp.where(d_iota == d_index, spin_d_ref[...][None, :], 0).astype(jnp.float32), axis=1, keepdims=True)
    spin_left = jnp.sum(jnp.where(c_iota == c_index, spin_c_ref[...][None, :], 0).astype(jnp.float32), axis=1, keepdims=True)
    factor = jnp.where(spin_left == spin_right, 0.5, 1.0)
    shift = (
        lax.broadcasted_iota(jnp.int32, (ROWS, kpiece), 0) - offset
        == lax.broadcasted_iota(jnp.int32, (ROWS, kpiece), 1)
    )
    placed = jnp.dot(
        shift.astype(jnp.float32).astype(jnp.bfloat16), tau_ref[...], preferred_element_type=jnp.float32
    )
    w_buf[...] = (placed * factor).astype(jnp.bfloat16)

    part_a = pl.ds(0, A_ROWS)

    def b_rows(u, z0, act):
        if u == 0:
            act(pl.ds(A_ROWS, ROWS - A_ROWS))
            return
        wide = (z0 == NZ - 1) & (kk == 1)

        @pl.when(wide)
        def _():
            act(pl.ds(A_ROWS, ROWS - A_ROWS))

        @pl.when(jnp.logical_not(wide))
        def _():
            act(pl.ds(A_ROWS, FEW - A_ROWS))

    def copy(src, dst, ssem, rsem, dev):
        return pltpu.make_async_remote_copy(
            src_ref=src, dst_ref=dst, send_sem=ssem, recv_sem=rsem, device_id=dev, device_id_type=MESH
        )

    def same(ref, ssem, rsem, dev):
        return copy(ref, ref, ssem, rsem, dev)

    def kind(u, i):
        return send_sem.at[u, i]

    def az(u, z0, way):
        return same(t_bufs[u].at[z0, xx, kk, part_a], kind(u, 0 if way > 0 else 7), az_r.at[u, z0], zdev(zz + way))

    def bz(u, z0, way, rows):
        return same(t_bufs[u].at[z0, :, kk, rows], kind(u, 1 if way > 0 else 8), bz_r.at[u, z0], zdev(zz + way))

    def turn(u, z0):
        return 1 - 2 * ((u + z0) % 2)

    def ax(u, z0, way):
        s = turn(u, z0) if way == 2 else 1 - 2 * way
        source = (xx - s + 4) % 4 if way == 2 else xx
        return same(t_bufs[u].at[z0, source, kk, part_a], kind(u, 2), ax_r.at[u, z0, way // 2], xdev((xx + s + 4) % 4))

    def ax_near(u, z0):
        return same(t_bufs[u].at[z0, 0:2, kk, part_a], kind(u, 2), ax_r.at[u, z0, 0], sib)

    def ax_far(u, z0):
        return same(t_bufs[u].at[z0, (xx + 2) % 4, kk, part_a], kind(u, 2), ax_r.at[u, z0, 1], sib)

    def bx(u, way, rows):
        s = turn(u, 0) if way == 2 else 1 - 2 * way
        source = (xx - s + 4) % 4 if way == 2 else xx
        return same(t_bufs[u].at[zz, source, kk, rows], kind(u, 3), bx_r.at[u, way // 2], xdev((xx + s + 4) % 4))

    def bx_near(u, rows):
        return same(t_bufs[u].at[zz, 0:2, kk, rows], kind(u, 3), bx_r.at[u, 0], sib)

    def bx_far(u, rows):
        return same(t_bufs[u].at[zz, (xx + 2) % 4, kk, rows], kind(u, 3), bx_r.at[u, 1], sib)

    def sb(u, z0):
        return same(t_bufs[u].at[z0, :, kk, 0:ROWS], kind(u, 4), sib_r.at[u, z0], sib)

    def sides(distance, act):
        for sign in (-1, 1):
            z0 = zz + sign * distance

            @pl.when((z0 >= 0) & (z0 < NZ))
            def _():
                act(z0, sign)

    def pass_on(sign, send):
        if sign <= 0:

            @pl.when(zz < NZ - 1)
            def _():
                send(1)

        if sign >= 0:

            @pl.when(zz > 0)
            def _():
                send(-1)

    def rows_at(distance, act):
        act(zz, 0) if distance == 0 else sides(distance, act)

    def z_step(u, distance):
        def act(z0, sign):
            az(u, z0, 0).wait_recv()
            pass_on(sign, lambda way: az(u, z0, way).start())
            ax(u, z0, 0).start()
            ax(u, z0, 1).start()

        sides(distance, act)

    def far_step(u, distance):
        def act(z0, sign):
            ax_near(u, z0).wait_recv()
            ax(u, z0, 2).start()

        rows_at(distance, act)

    def row_step(u, distance):
        def act(z0, sign):
            def hop(rows):
                (bx_far(u, rows) if distance == 0 else bz(u, z0, 0, rows)).wait_recv()
                pass_on(sign, lambda way: bz(u, z0, way, rows).start())

            b_rows(u, z0, hop)
            ax_far(u, z0).wait_recv()
            sb(u, z0).start()

        rows_at(distance, act)

    def own_fill(u):
        j, cores = UNITS[u]
        n, lanes = len(cores), LANES[u]
        q = lax.broadcasted_iota(jnp.int32, (1, lanes), 1)
        if u == LAST:
            q_y, q_x, q_h, q_z, q_k = q // 32, q // 8 % 4, q // 4 % 2, q % 4, cores[0]
        else:
            q_y, q_h, q_z, q_k, q_x = q // (32 * n), q // (16 * n) % 2, q // (4 * n) % 4, q // 4 % n + cores[0], q % 4
        pair = (q_h * 4 + q_y) * 128 + (q_x * 8 + q_z * 2 + q_k) * 4 + j
        pick = lax.broadcasted_iota(jnp.int32, (tau_ref.shape[1], lanes), 0) == pair
        block = jnp.dot(
            w_buf[...], pick.astype(jnp.float32).astype(jnp.bfloat16), preferred_element_type=jnp.float32
        )
        t_bufs[u][zz, xx, kk, 0:ROWS, :] = block.astype(jnp.bfloat16)

    def own_send(u):
        pass_on(0, lambda way: az(u, zz, way).start())
        b_rows(u, zz, lambda rows: (bx(u, 0, rows).start(), bx(u, 1, rows).start()))
        ax(u, zz, 0).start()
        ax(u, zz, 1).start()

    def bx_step(u):
        b_rows(u, zz, lambda rows: (bx_near(u, rows).wait_recv(), bx(u, 2, rows).start()))

    def turn_v(z0):
        def one(i, carry):
            t = i // NK * (NZ * NK) + z0 * NK + i % NK
            first = pl.multiple_of((kpiece * t) // 16 * 16, 16)
            lanes = pl.ds(pl.multiple_of((z0 * NX * NK + i) * PAD, PAD), PAD)
            for s in range(v_buf.shape[0]):
                vt_buf[s * 128 : (s + 1) * 128, lanes] = v_buf[s, pl.ds(first, PAD), :].T
            return carry

        lax.fori_loop(0, NX * NK, one, 0)

    def multiply(u, distance):
        depth = NX * NK * PAD

        def act(z0, sign):
            t_bufs_row = t_bufs[u].at[z0]
            same(t_bufs_row.at[:, 1 - kk, 0:ROWS], kind(u, 4), sib_r.at[u, z0], sib).wait_recv()
            if distance == 0:
                accs[u][...] = jnp.zeros(accs[u].shape, jnp.float32)

            def one(i, carry):
                size = depth // 2
                part = vt_buf[:, pl.ds(pl.multiple_of(z0 * depth + i * size, size), size)]
                block = t_bufs_row[pl.ds(i * 2, 2)].reshape(size, LANES[u])
                accs[u][...] += jnp.dot(part, block, preferred_element_type=jnp.float32)
                return carry

            lax.fori_loop(0, 2, one, 0)

        rows_at(distance, act)

    def y_step(u):
        r_buf = r_bufs[u]
        quarter = r_buf.shape[0] // NY
        for half in range(LANES[u] // 128):
            lanes = slice(half * 128, half * 128 + 128)
            for s in range(v_buf.shape[0]):
                rows = slice(s * 128, s * 128 + 128)
                r_buf[lanes, rows] = (accs[u][rows, lanes] * scales_ref[s]).T
        if u == LAST:
            for turn, step in ((2, 2), (2, 1), (2, 3), (1, 2), (3, 2), (1, 1), (3, 3), (1, 3), (3, 1)):
                plane_send(u, step, turn)
            for step in (2, 1, 3):
                plane_send(u, step, 0)
                plane_send(u, 0, step)
            return
        for step in (2, 1, 3):
            other = (yy + step) % NY
            rows = pl.ds(pl.multiple_of(other * quarter, quarter), quarter)
            copy(r_buf.at[rows], y_bufs[u].at[3 - step], kind(u, 5), y_r.at[u], ydev(other)).start()

    def plane_send(u, step, turn):
        y, x = (yy + step) % NY, (xx + turn) % NX
        rows = pl.ds(pl.multiple_of((y * NX + x) * 8, 8), 8)
        copy(r_bufs[u].at[rows], y_bufs[u].at[yy * NX + xx], kind(u, 5), y_r.at[u], plane(y, x)).start()

    def last_z(u):
        r_buf, y_buf, q_buf, z_buf = r_bufs[u], y_bufs[u], q_bufs[u], z_bufs[u]
        core = UNITS[u][1][0]
        mine = yy * NX + xx
        y_buf[mine] = r_buf[pl.ds(pl.multiple_of(mine * 8, 8), 8), :]
        same(y_buf.at[0 : NY * NX - 1], kind(u, 5), y_r.at[u], sib).wait_recv()
        for x in range(NX):
            total = y_buf[x] + y_buf[NX + x] + y_buf[2 * NX + x] + y_buf[3 * NX + x]
            for other in range(NH * NZ):
                q_buf[other, x : x + 1, :] = total[other : other + 1, :]

        def send(other):
            copy(q_buf.at[other], z_buf.at[place * NK + kk], kind(u, 6), z_r.at[u], ring(other, core)).start()

        for step in (4, 3, 5, 2, 6, 1, 7):
            send((place + step) % (NH * NZ))

        @pl.when(kk == core)
        def _():
            z_buf[place * NK + kk] = q_buf[place]

        @pl.when(kk != core)
        def _():
            send(place)

    def last_own(u):
        z_buf = z_bufs[u]
        j, (core,) = UNITS[u]

        @pl.when(kk == core)
        def _():
            same(z_buf.at[0 : NH * NZ * NK - 1], kind(u, 6), z_r.at[u], sib).wait_recv()
            for z in range(NZ):
                for k in range(NK):
                    both = z_buf[z * NK + k] + z_buf[(NZ + z) * NK + k]
                    for x in range(NX):
                        own_buf[j, x * NK + k, z : z + 1, :] = both[x : x + 1, :]

    def finish(p):
        width = ab_ref.shape[1]
        owned = own_buf[p].reshape(NX * NK * NZ, own_buf.shape[3])
        residual = jnp.zeros(ab_ref.shape, jnp.float32)
        for s in range(v_buf.shape[0]):
            residual += jnp.dot(
                pick_buf[s],
                owned[:, s * width : (s + 1) * width],
                precision=lax.Precision.HIGHEST,
                preferred_element_type=jnp.float32,
            )
        out_ref[:, p, :] = residual / (ab_ref[...] - pair_ref[p])

    def x_done(u):
        j, cores = UNITS[u]
        for core in range(NK):
            if core in cores:

                @pl.when(kk == core)
                def _():
                    same(own_buf.at[j, 0 : NX * NK - 1], kind(u, 9), x_r.at[u], sib).wait_recv()

        if len(cores) == NK:
            sent(s_buf.at[j, 0 : NX * NK - 1], kind(u, 9))
            finish(j)
            return

        @pl.when(kk == cores[0])
        def _():
            sent(s_buf.at[j, 0 : NX - 1], kind(u, 9))

        @pl.when(kk != cores[0])
        def _():
            sent(s_buf.at[j, 0:NX], kind(u, 9))

    def zs_step(u):
        r_buf, y_buf, q_buf, z_buf = r_bufs[u], y_bufs[u], q_bufs[u], z_bufs[u]
        quarter = r_buf.shape[0] // NY
        rows = q_buf.shape[1]
        same(y_buf, kind(u, 5), y_r.at[u], sib).wait_recv()
        mine = r_buf[pl.ds(pl.multiple_of(yy * quarter, quarter), quarter), :]
        total = mine + y_buf[0] + y_buf[1] + y_buf[2]
        for other in range(NH * NZ):
            q_buf[other] = total[other * rows : (other + 1) * rows, :]
        z_buf[place] = q_buf[place]
        for step in (4, 3, 5, 2, 6, 1, 7):
            other = (place + step) % (NH * NZ)
            copy(q_buf.at[other], z_buf.at[place], kind(u, 6), z_r.at[u], ring(other)).start()

    def xs_step(u):
        z_buf = z_bufs[u]
        j, cores = UNITS[u]
        same(z_buf.at[0 : NH * NZ - 1], kind(u, 6), z_r.at[u], sib).wait_recv()
        for z in range(NZ):
            both = z_buf[z] + z_buf[NZ + z]
            for i, core in enumerate(cores):
                for x in range(NX):
                    s_buf[j, core * NX + x, z : z + 1, :] = both[i * NX + x : i * NX + x + 1, :]

        def send(core, step):
            other = (xx + step) % NX
            copy(s_buf.at[j, core * NX + other], own_buf.at[j, xx * NK + kk], kind(u, 9), x_r.at[u], xdev(other, core)).start()

        for core in cores:

            @pl.when(kk == core)
            def _():
                for step in (2, 1, 3):
                    send(core, step)
                own_buf[j, xx * NK + kk] = s_buf[j, core * NX + xx]

            @pl.when(kk != core)
            def _():
                for step in (2, 1, 3, 0):
                    send(core, step)

    def sent(ref, sem):
        same(ref, sem, sem, sib).wait_send()

    def gather_sent(u):
        t_buf = t_bufs[u]
        sent(t_buf.at[0:3, :, 0, part_a], kind(u, 2))
        b_rows(u, zz, lambda rows: sent(t_buf.at[0:3, 0, 0, rows], kind(u, 3)))
        sent(t_buf.at[:, :, 0, 0:ROWS], kind(u, 4))

        for v in range(NZ):

            @pl.when(zz == v)
            def _():
                ups, downs = v + 1 if v < NZ - 1 else 0, NZ - v if v > 0 else 0
                few = pl.ds(A_ROWS, (ROWS if u == 0 else FEW) - A_ROWS)
                if ups:
                    sent(t_buf.at[0, 0:ups, 0, part_a], kind(u, 0))
                    sent(t_buf.at[:, 0:ups, 0, few], kind(u, 1))
                if downs:
                    sent(t_buf.at[0, 0:downs, 0, part_a], kind(u, 7))
                if downs and u == 0:
                    sent(t_buf.at[:, 0:downs, 0, few], kind(u, 8))
                elif downs:

                    @pl.when(kk == 1)
                    def _():
                        sent(t_buf.at[0, :, 0, 0 : (FEW - A_ROWS) * downs + ROWS - FEW], kind(u, 8))

                    @pl.when(kk != 1)
                    def _():
                        sent(t_buf.at[:, 0:downs, 0, few], kind(u, 8))

    def slot_pick():
        slots, owners = v_buf.shape[0], NX * NK * NZ
        g = lax.broadcasted_iota(jnp.int32, (owners, slots * owners), 1)
        t = lax.broadcasted_iota(jnp.int32, (owners, slots * owners), 0)
        held = jnp.where(g // slots == t, 1.0, 0.0).astype(jnp.bfloat16)
        counts = jnp.broadcast_to(counts_ref[...][None, :], (8, owners)).astype(jnp.float32).astype(jnp.bfloat16)
        count = jnp.dot(counts, held, preferred_element_type=jnp.float32)
        ids = jnp.broadcast_to(ids_ref[...][None, :], count.shape).astype(jnp.float32)
        slot = lax.broadcasted_iota(jnp.int32, count.shape, 1) % slots
        ids = jnp.where(slot.astype(jnp.float32) < count, ids, -1.0).astype(jnp.bfloat16)
        g = lax.broadcasted_iota(jnp.int32, (slots * owners, owners), 0)
        r = lax.broadcasted_iota(jnp.int32, (slots * owners, owners), 1)
        t = r // (NK * NZ) * (NK * NZ) + r % NZ * NK + r // NZ % NK
        j = lax.broadcasted_iota(jnp.int32, (slots * owners, owners), 0).astype(jnp.float32)
        for s in range(slots):
            order = jnp.where(g == t * slots + s, 1.0, 0.0).astype(jnp.bfloat16)
            mine = jnp.dot(ids, order, preferred_element_type=jnp.float32)
            pick_buf[s] = jnp.where(mine[0:1, :] == j, 1.0, 0.0)

    own_fill(0)
    pl.semaphore_wait(barrier, (NX - 1) + (NY - 1) * NX + (NH * NZ - 1) * NK + NX + 2)
    gives, gets = tile % 16 != 15, tile % 16 != 0
    edge = copy(w_buf.at[FEW:ROWS], edge_buf, edge_sem.at[0], edge_sem.at[1], (layer, (tile + 1) % tiles))

    @pl.when(gives)
    def _():
        edge.start()

    own_send(0)

    @pl.when(gives)
    def _():
        edge.wait_send()
        w_buf[FEW:ROWS, :] = jnp.zeros((ROWS - FEW, w_buf.shape[1]), w_buf.dtype)

    @pl.when(gets)
    def _():
        edge.wait_recv()
        both = w_buf[0 : ROWS - FEW, :].astype(jnp.float32) + edge_buf[...].astype(jnp.float32)
        w_buf[0 : ROWS - FEW, :] = both.astype(w_buf.dtype)

    own_fill(1)

    for tick in range(COUNT + 8):

        def at(stage, act):
            if 0 <= tick - stage < COUNT:
                act(tick - stage)

        at(-1, own_send)
        at(1, lambda u: (bx_step(u), z_step(u, 1), far_step(u, 0)))
        at(3, lambda u: multiply(u, 0))
        at(2, lambda u: (row_step(u, 0), far_step(u, 1), z_step(u, 2)))
        at(4, lambda u: multiply(u, 1))
        at(3, lambda u: (row_step(u, 1), far_step(u, 2), z_step(u, 3)))
        at(5, lambda u: multiply(u, 2))
        at(4, lambda u: (row_step(u, 2), far_step(u, 3)))
        at(5, lambda u: row_step(u, 3))
        at(6, lambda u: multiply(u, 3))
        at(6, y_step)
        at(7, lambda u: last_z(u) if u == LAST else zs_step(u))
        at(8, lambda u: last_own(u) if u == LAST else xs_step(u))
        at(9, lambda u: None if u == LAST else x_done(u))
        if tick == 1:
            v_copy.wait()
        if 1 <= tick <= NZ:
            turn_v((zz + (0, 1, 3, 2)[tick - 1]) % NZ)
        at(-2, own_fill)
        if tick == 0:
            def clear(step, carry):
                for t_buf in t_bufs:
                    t_buf[step // 8, step // 2 % 4, step % 2, ROWS:, :] = jnp.zeros((PAD - ROWS, t_buf.shape[-1]), jnp.bfloat16)

                @pl.when((step % 2 == kk) & jnp.logical_not((step // 8 == NZ - 1) & (kk == 1)))
                def _():
                    for t_buf in t_bufs[1:]:
                        t_buf[step // 8, step // 2 % 4, step % 2, FEW:ROWS, :] = jnp.zeros((ROWS - FEW, t_buf.shape[-1]), jnp.bfloat16)

                return carry

            lax.fori_loop(0, NX * NZ * NK, clear, 0)
            slot_pick()
        at(6, gather_sent)

    finish(UNITS[LAST][0])
    for u in range(LAST):
        sent(r_bufs[u].at[0 : r_bufs[u].shape[0] // 4 * 3], kind(u, 5))
        sent(q_bufs[u].at[0 : NH * NZ - 1], kind(u, 6))
    sent(r_bufs[LAST].at[0 : (NY * NX - 1) * 8], kind(LAST, 5))

    @pl.when(kk == UNITS[LAST][1][0])
    def _():
        sent(q_bufs[LAST].at[0 : NH * NZ - 1], kind(LAST, 6))

    @pl.when(kk != UNITS[LAST][1][0])
    def _():
        sent(q_bufs[LAST], kind(LAST, 6))


def local(tau, vvvv, scales, tile_ids, counts, spin_c, spin_d, pair_energy, ab_energy):
    slots, width, klayer = vvvv.shape
    pairs, kpiece = tau.shape
    ntile = lax.axis_size("tile")
    nlayer = lax.axis_size("layer")
    own_pairs = pairs // (nlayer * ntile)
    all_slots = slots * ntile
    vmem = pl.BlockSpec(memory_space=pltpu.VMEM)
    bf16, f32 = jnp.bfloat16, jnp.float32
    dma = pltpu.SemaphoreType.DMA
    columns = slots * width
    smem = pl.BlockSpec(memory_space=pltpu.SMEM)
    amplitudes = pl.pallas_call(
        ladder_kernel,
        out_shape=jax.ShapeDtypeStruct((all_slots, own_pairs, width), f32),
        in_specs=[vmem, pl.BlockSpec(memory_space=pl.ANY), smem, vmem, vmem, vmem, vmem, smem, vmem],
        out_specs=vmem,
        scratch_shapes=[
            pltpu.VMEM((own_pairs, NX * NK, NZ, columns), f32),
            pltpu.VMEM((slots, all_slots, ntile), f32),
            [pltpu.VMEM((NZ, NX, NK, PAD, lanes), bf16) for lanes in LANES],
            pltpu.VMEM((slots, klayer + 16, width), bf16),
            pltpu.VMEM((columns, ntile * PAD), bf16),
            pltpu.VMEM((ROWS, pairs), bf16),
            pltpu.VMEM((ROWS - FEW, pairs), bf16),
            [pltpu.VMEM((columns, lanes), f32) for lanes in LANES],
            [pltpu.VMEM((lanes, columns), f32) for lanes in LANES],
            [pltpu.VMEM((NY - 1, lanes // NY, columns), f32) for lanes in LANES[:LAST]]
            + [pltpu.VMEM((NY * NX, NH * NZ, columns), f32)],
            [pltpu.VMEM((NH * NZ, lanes // 32, columns), f32) for lanes in LANES],
            [pltpu.VMEM((NH * NZ, lanes // 32, columns), f32) for lanes in LANES[:LAST]]
            + [pltpu.VMEM((NH * NZ * NK, NX, columns), f32)],
            pltpu.VMEM((own_pairs, NX * NK, NZ, columns), f32),
            dma,
            dma((2,)),
            dma((COUNT, 10)),
            dma((COUNT, NZ)),
            dma((COUNT, NZ, 2)),
            dma((COUNT, 2)),
            dma((COUNT, NZ)),
            dma((COUNT, NZ)),
            dma((COUNT,)),
            dma((COUNT,)),
            dma((COUNT,)),
        ],
        compiler_params=pltpu.CompilerParams(
            collective_id=0, has_side_effects=True, vmem_limit_bytes=56 * 1024 * 1024
        ),
        name="ladder",
    )(tau.T, jnp.swapaxes(vvvv, 1, 2), scales, spin_c, spin_d, tile_ids, counts, pair_energy, ab_energy)
    return jnp.swapaxes(amplitudes, 0, 1).reshape(own_pairs, all_slots * width)


def solution(mesh):
    placed = (
        P(None, ("layer", "tile")),
        P("tile", None, "layer"),
        P("tile"),
        P(),
        P(),
        P(),
        P(),
        P(("layer", "tile")),
        P(),
    )
    return jax.shard_map(
        local, mesh=mesh, in_specs=placed, out_specs=P(("layer", "tile"), None), check_vma=False
    )
```

```python
import functools

import jax
import jax.numpy as jnp
from jax import lax
from jax.experimental import pallas as pl
from jax.experimental.pallas import tpu as pltpu
from jax.sharding import PartitionSpec as P

MESH = pl.DeviceIdType.MESH

NX, NZ, NK, NY, NH = 4, 4, 2, 4, 2
UNITS = ((0, (0, 1)), (1, (0, 1)), (2, (0, 1)), (3, (0,)), (3, (1,)))
LANES = tuple(128 * len(cores) for _, cores in UNITS)
COUNT = len(UNITS)
DIRECT = (4,)
LAST = COUNT - 1
ROWS = 240
FEW = 224
PAD = 256
A_ROWS = 176


def ladder_kernel(
    tau_ref,
    v_hbm,
    scales_ref,
    spin_c_ref,
    spin_d_ref,
    ids_ref,
    counts_ref,
    pair_ref,
    ab_ref,
    out_ref,
    own_buf,
    pick_buf,
    t_bufs,
    v_buf,
    vt_buf,
    w_buf,
    edge_buf,
    accs,
    r_bufs,
    y_bufs,
    q_bufs,
    z_bufs,
    s_buf,
    v_sem,
    edge_sem,
    send_sem,
    az_r,
    ax_r,
    bx_r,
    bz_r,
    sib_r,
    y_r,
    z_r,
    x_r,
):
    layer = lax.axis_index("layer")
    tile = lax.axis_index("tile")
    xx, zz, kk = tile // 8, (tile // 2) % 4, tile % 2
    hh, yy = layer // 4, layer % 4
    kpiece = tau_ref.shape[0]
    klayer = v_hbm.shape[1]
    virtual = spin_d_ref.shape[0]
    panel = spin_c_ref.shape[0]

    place = hh * NZ + zz

    def xdev(x, core=None):
        return (layer, x * 8 + zz * 2 + (kk if core is None else core))

    def zdev(z):
        return (layer, xx * 8 + z * 2 + kk)

    sib = xdev(xx, 1 - kk)

    def ydev(y):
        return (hh * 4 + y, tile)

    def ring(other):
        return (other // NZ * 4 + yy, xx * 8 + other % NZ * 2 + kk)

    barrier = pltpu.get_barrier_semaphore()

    def greet(dev):
        pl.semaphore_signal(barrier, inc=1, device_id=dev, device_id_type=MESH)

    for step in range(1, NH * NZ):
        greet(ring((place + step) % (NH * NZ)))
    for step in range(1, NY):
        greet(ydev((yy + step) % NY))
    for step in range(1, NX):
        greet(xdev((xx + step) % NX))
    for step in range(NX):
        greet(xdev((xx + step) % NX, 1 - kk))
    tiles = NX * NZ * NK
    greet((layer, (tile + 1) % tiles))
    greet((layer, (tile + tiles - 1) % tiles))

    v_copy = pltpu.make_async_copy(v_hbm, v_buf.at[:, pl.ds(0, klayer)], v_sem)
    v_copy.start()
    v_buf[:, klayer:, :] = jnp.zeros((v_buf.shape[0], v_buf.shape[1] - klayer, 128), v_buf.dtype)

    start = (kpiece * tile) // 16 * 16
    offset = kpiece * tile - start
    base = layer * klayer + start
    c_first = base // virtual
    d_first = base - c_first * virtual
    row = lax.broadcasted_iota(jnp.int32, (ROWS, 1), 0)
    d_index = row + d_first
    over = d_index >= virtual
    d_index = jnp.where(over, d_index - virtual, d_index)
    c_index = jnp.where(over, c_first + 1, c_first)
    d_iota = lax.broadcasted_iota(jnp.int32, (ROWS, virtual), 1)
    c_iota = lax.broadcasted_iota(jnp.int32, (ROWS, panel), 1)
    spin_right = jnp.sum(jnp.where(d_iota == d_index, spin_d_ref[...][None, :], 0).astype(jnp.float32), axis=1, keepdims=True)
    spin_left = jnp.sum(jnp.where(c_iota == c_index, spin_c_ref[...][None, :], 0).astype(jnp.float32), axis=1, keepdims=True)
    factor = jnp.where(spin_left == spin_right, 0.5, 1.0)
    shift = (
        lax.broadcasted_iota(jnp.int32, (ROWS, kpiece), 0) - offset
        == lax.broadcasted_iota(jnp.int32, (ROWS, kpiece), 1)
    )
    placed = jnp.dot(
        shift.astype(jnp.float32).astype(jnp.bfloat16), tau_ref[...], preferred_element_type=jnp.float32
    )
    w_buf[...] = (placed * factor).astype(jnp.bfloat16)

    part_a = pl.ds(0, A_ROWS)

    def b_rows(u, z0, act):
        if u == 0:
            act(pl.ds(A_ROWS, ROWS - A_ROWS))
            return
        wide = (z0 == NZ - 1) & (kk == 1)

        @pl.when(wide)
        def _():
            act(pl.ds(A_ROWS, ROWS - A_ROWS))

        @pl.when(jnp.logical_not(wide))
        def _():
            act(pl.ds(A_ROWS, FEW - A_ROWS))

    def copy(src, dst, ssem, rsem, dev):
        return pltpu.make_async_remote_copy(
            src_ref=src, dst_ref=dst, send_sem=ssem, recv_sem=rsem, device_id=dev, device_id_type=MESH
        )

    def same(ref, ssem, rsem, dev):
        return copy(ref, ref, ssem, rsem, dev)

    def kind(u, i):
        return send_sem.at[u, i]

    def az(u, z0, way):
        return same(t_bufs[u].at[z0, xx, kk, part_a], kind(u, 0 if way > 0 else 7), az_r.at[u, z0], zdev(zz + way))

    def bz(u, z0, way, rows):
        return same(t_bufs[u].at[z0, :, kk, rows], kind(u, 1 if way > 0 else 8), bz_r.at[u, z0], zdev(zz + way))

    def turn(u, z0):
        return 1 - 2 * ((u + z0) % 2)

    def ax(u, z0, way):
        s = turn(u, z0) if way == 2 else 1 - 2 * way
        source = (xx - s + 4) % 4 if way == 2 else xx
        return same(t_bufs[u].at[z0, source, kk, part_a], kind(u, 2), ax_r.at[u, z0, way // 2], xdev((xx + s + 4) % 4))

    def ax_near(u, z0):
        return same(t_bufs[u].at[z0, 0:2, kk, part_a], kind(u, 2), ax_r.at[u, z0, 0], sib)

    def ax_far(u, z0):
        return same(t_bufs[u].at[z0, (xx + 2) % 4, kk, part_a], kind(u, 2), ax_r.at[u, z0, 1], sib)

    def bx(u, way, rows):
        s = turn(u, 0) if way == 2 else 1 - 2 * way
        source = (xx - s + 4) % 4 if way == 2 else xx
        return same(t_bufs[u].at[zz, source, kk, rows], kind(u, 3), bx_r.at[u, way // 2], xdev((xx + s + 4) % 4))

    def bx_near(u, rows):
        return same(t_bufs[u].at[zz, 0:2, kk, rows], kind(u, 3), bx_r.at[u, 0], sib)

    def bx_far(u, rows):
        return same(t_bufs[u].at[zz, (xx + 2) % 4, kk, rows], kind(u, 3), bx_r.at[u, 1], sib)

    def sb(u, z0):
        return same(t_bufs[u].at[z0, :, kk, 0:ROWS], kind(u, 4), sib_r.at[u, z0], sib)

    def sides(distance, act):
        for sign in (-1, 1):
            z0 = zz + sign * distance

            @pl.when((z0 >= 0) & (z0 < NZ))
            def _():
                act(z0, sign)

    def pass_on(sign, send):
        if sign <= 0:

            @pl.when(zz < NZ - 1)
            def _():
                send(1)

        if sign >= 0:

            @pl.when(zz > 0)
            def _():
                send(-1)

    def rows_at(distance, act):
        act(zz, 0) if distance == 0 else sides(distance, act)

    def z_step(u, distance):
        def act(z0, sign):
            az(u, z0, 0).wait_recv()
            if u not in DIRECT:
                pass_on(sign, lambda way: az(u, z0, way).start())
            ax(u, z0, 0).start()
            ax(u, z0, 1).start()

        sides(distance, act)

    def far_step(u, distance):
        def act(z0, sign):
            ax_near(u, z0).wait_recv()
            ax(u, z0, 2).start()

        rows_at(distance, act)

    def row_step(u, distance):
        def act(z0, sign):
            def hop(rows):
                (bx_far(u, rows) if distance == 0 else bz(u, z0, 0, rows)).wait_recv()
                if u not in DIRECT:
                    pass_on(sign, lambda way: bz(u, z0, way, rows).start())
                elif distance == 0:
                    for d in (3, 2, 1):
                        sides(d, lambda _, side: bz(u, zz, side * d, rows).start())

            b_rows(u, z0, hop)
            ax_far(u, z0).wait_recv()
            sb(u, z0).start()

        rows_at(distance, act)

    def own_fill(u):
        j, cores = UNITS[u]
        n, lanes = len(cores), LANES[u]
        q = lax.broadcasted_iota(jnp.int32, (1, lanes), 1)
        q_y, q_h, q_z, q_k, q_x = q // (32 * n), q // (16 * n) % 2, q // (4 * n) % 4, q // 4 % n + cores[0], q % 4
        pair = (q_h * 4 + q_y) * 128 + (q_x * 8 + q_z * 2 + q_k) * 4 + j
        pick = lax.broadcasted_iota(jnp.int32, (tau_ref.shape[1], lanes), 0) == pair
        block = jnp.dot(
            w_buf[...], pick.astype(jnp.float32).astype(jnp.bfloat16), preferred_element_type=jnp.float32
        )
        t_bufs[u][zz, xx, kk, 0:ROWS, :] = block.astype(jnp.bfloat16)

    def own_send(u):
        if u in DIRECT:
            for d in (3, 2, 1):
                sides(d, lambda z0, sign: az(u, zz, sign * d).start())
        else:
            pass_on(0, lambda way: az(u, zz, way).start())
        b_rows(u, zz, lambda rows: (bx(u, 0, rows).start(), bx(u, 1, rows).start()))
        ax(u, zz, 0).start()
        ax(u, zz, 1).start()

    def bx_step(u):
        b_rows(u, zz, lambda rows: (bx_near(u, rows).wait_recv(), bx(u, 2, rows).start()))

    def turn_v(z0):
        def one(i, carry):
            t = i // NK * (NZ * NK) + z0 * NK + i % NK
            first = pl.multiple_of((kpiece * t) // 16 * 16, 16)
            lanes = pl.ds(pl.multiple_of((z0 * NX * NK + i) * PAD, PAD), PAD)
            for s in range(v_buf.shape[0]):
                vt_buf[s * 128 : (s + 1) * 128, lanes] = v_buf[s, pl.ds(first, PAD), :].T
            return carry

        lax.fori_loop(0, NX * NK, one, 0)

    def multiply(u, distance):
        depth = NX * NK * PAD

        def act(z0, sign):
            t_bufs_row = t_bufs[u].at[z0]
            same(t_bufs_row.at[:, 1 - kk, 0:ROWS], kind(u, 4), sib_r.at[u, z0], sib).wait_recv()
            if distance == 0:
                accs[u][...] = jnp.zeros(accs[u].shape, jnp.float32)

            def one(i, carry):
                size = depth // 2
                part = vt_buf[:, pl.ds(pl.multiple_of(z0 * depth + i * size, size), size)]
                block = t_bufs_row[pl.ds(i * 2, 2)].reshape(size, LANES[u])
                accs[u][...] += jnp.dot(part, block, preferred_element_type=jnp.float32)
                return carry

            lax.fori_loop(0, 2, one, 0)

        rows_at(distance, act)

    def y_step(u):
        r_buf = r_bufs[u]
        quarter = r_buf.shape[0] // NY
        for half in range(LANES[u] // 128):
            lanes = slice(half * 128, half * 128 + 128)
            for s in range(v_buf.shape[0]):
                rows = slice(s * 128, s * 128 + 128)
                r_buf[lanes, rows] = (accs[u][rows, lanes] * scales_ref[s]).T
        for step in (2, 1, 3):
            other = (yy + step) % NY
            rows = pl.ds(pl.multiple_of(other * quarter, quarter), quarter)
            copy(r_buf.at[rows], y_bufs[u].at[3 - step], kind(u, 5), y_r.at[u], ydev(other)).start()

    def finish(p):
        width = ab_ref.shape[1]
        owned = own_buf[p].reshape(NX * NK * NZ, own_buf.shape[3])
        residual = jnp.zeros(ab_ref.shape, jnp.float32)
        for s in range(v_buf.shape[0]):
            residual += jnp.dot(
                pick_buf[s],
                owned[:, s * width : (s + 1) * width],
                precision=lax.Precision.HIGHEST,
                preferred_element_type=jnp.float32,
            )
        out_ref[:, p, :] = residual / (ab_ref[...] - pair_ref[p])

    def x_done(u):
        j, cores = UNITS[u]
        for core in range(NK):
            if core in cores:

                @pl.when(kk == core)
                def _():
                    same(own_buf.at[j, 0 : NX * NK - 1], kind(u, 9), x_r.at[u], sib).wait_recv()

        if len(cores) == NK:
            sent(s_buf.at[j, 0 : NX * NK - 1], kind(u, 9))
            finish(j)
            return

        @pl.when(kk == cores[0])
        def _():
            sent(s_buf.at[j, 0 : NX - 1], kind(u, 9))

        @pl.when(kk != cores[0])
        def _():
            sent(s_buf.at[j, 0:NX], kind(u, 9))

        if u != LAST and all(place != j for place, _ in UNITS[u + 1 :]):
            finish(j)

    def zs_step(u):
        r_buf, y_buf, q_buf, z_buf = r_bufs[u], y_bufs[u], q_bufs[u], z_bufs[u]
        quarter = r_buf.shape[0] // NY
        rows = q_buf.shape[1]
        same(y_buf, kind(u, 5), y_r.at[u], sib).wait_recv()
        mine = r_buf[pl.ds(pl.multiple_of(yy * quarter, quarter), quarter), :]
        total = mine + y_buf[0] + y_buf[1] + y_buf[2]
        for other in range(NH * NZ):
            q_buf[other] = total[other * rows : (other + 1) * rows, :]
        z_buf[place] = q_buf[place]
        for step in (4, 3, 5, 2, 6, 1, 7):
            other = (place + step) % (NH * NZ)
            copy(q_buf.at[other], z_buf.at[place], kind(u, 6), z_r.at[u], ring(other)).start()

    def xs_step(u):
        z_buf = z_bufs[u]
        j, cores = UNITS[u]
        same(z_buf.at[0 : NH * NZ - 1], kind(u, 6), z_r.at[u], sib).wait_recv()
        for z in range(NZ):
            both = z_buf[z] + z_buf[NZ + z]
            for i, core in enumerate(cores):
                for x in range(NX):
                    s_buf[j, core * NX + x, z : z + 1, :] = both[i * NX + x : i * NX + x + 1, :]

        def send(core, step):
            other = (xx + step) % NX
            copy(s_buf.at[j, core * NX + other], own_buf.at[j, xx * NK + kk], kind(u, 9), x_r.at[u], xdev(other, core)).start()

        for core in cores:

            @pl.when(kk == core)
            def _():
                for step in (2, 1, 3):
                    send(core, step)
                own_buf[j, xx * NK + kk] = s_buf[j, core * NX + xx]

            @pl.when(kk != core)
            def _():
                for step in (2, 1, 3, 0):
                    send(core, step)

    def sent(ref, sem):
        same(ref, sem, sem, sib).wait_send()

    def gather_sent(u):
        t_buf = t_bufs[u]
        sent(t_buf.at[0:3, :, 0, part_a], kind(u, 2))
        b_rows(u, zz, lambda rows: sent(t_buf.at[0:3, 0, 0, rows], kind(u, 3)))
        sent(t_buf.at[:, :, 0, 0:ROWS], kind(u, 4))

        for v in range(NZ):

            @pl.when(zz == v)
            def _():
                if u in DIRECT:
                    for count, i in ((NZ - 1 - v, 0), (v, 7)):
                        if count:
                            sent(t_buf.at[0, 0:count, 0, part_a], kind(u, i))
                            b_rows(u, v, lambda rows: sent(t_buf.at[:, 0:count, 0, rows], kind(u, i + 1)))
                    return
                ups, downs = v + 1 if v < NZ - 1 else 0, NZ - v if v > 0 else 0
                few = pl.ds(A_ROWS, (ROWS if u == 0 else FEW) - A_ROWS)
                if ups:
                    sent(t_buf.at[0, 0:ups, 0, part_a], kind(u, 0))
                    sent(t_buf.at[:, 0:ups, 0, few], kind(u, 1))
                if downs:
                    sent(t_buf.at[0, 0:downs, 0, part_a], kind(u, 7))
                if downs and u == 0:
                    sent(t_buf.at[:, 0:downs, 0, few], kind(u, 8))
                elif downs:

                    @pl.when(kk == 1)
                    def _():
                        sent(t_buf.at[0, :, 0, 0 : (FEW - A_ROWS) * downs + ROWS - FEW], kind(u, 8))

                    @pl.when(kk != 1)
                    def _():
                        sent(t_buf.at[:, 0:downs, 0, few], kind(u, 8))

    def slot_pick():
        slots, owners = v_buf.shape[0], NX * NK * NZ
        g = lax.broadcasted_iota(jnp.int32, (owners, slots * owners), 1)
        t = lax.broadcasted_iota(jnp.int32, (owners, slots * owners), 0)
        held = jnp.where(g // slots == t, 1.0, 0.0).astype(jnp.bfloat16)
        counts = jnp.broadcast_to(counts_ref[...][None, :], (8, owners)).astype(jnp.float32).astype(jnp.bfloat16)
        count = jnp.dot(counts, held, preferred_element_type=jnp.float32)
        ids = jnp.broadcast_to(ids_ref[...][None, :], count.shape).astype(jnp.float32)
        slot = lax.broadcasted_iota(jnp.int32, count.shape, 1) % slots
        ids = jnp.where(slot.astype(jnp.float32) < count, ids, -1.0).astype(jnp.bfloat16)
        g = lax.broadcasted_iota(jnp.int32, (slots * owners, owners), 0)
        r = lax.broadcasted_iota(jnp.int32, (slots * owners, owners), 1)
        t = r // (NK * NZ) * (NK * NZ) + r % NZ * NK + r // NZ % NK
        j = lax.broadcasted_iota(jnp.int32, (slots * owners, owners), 0).astype(jnp.float32)
        for s in range(slots):
            order = jnp.where(g == t * slots + s, 1.0, 0.0).astype(jnp.bfloat16)
            mine = jnp.dot(ids, order, preferred_element_type=jnp.float32)
            pick_buf[s] = jnp.where(mine[0:1, :] == j, 1.0, 0.0)

    own_fill(0)
    pl.semaphore_wait(barrier, (NX - 1) + (NY - 1) + (NH * NZ - 1) + NX + 2)
    gives, gets = tile % 16 != 15, tile % 16 != 0
    edge = copy(w_buf.at[FEW:ROWS], edge_buf, edge_sem.at[0], edge_sem.at[1], (layer, (tile + 1) % tiles))

    @pl.when(gives)
    def _():
        edge.start()

    own_send(0)

    @pl.when(gives)
    def _():
        edge.wait_send()
        w_buf[FEW:ROWS, :] = jnp.zeros((ROWS - FEW, w_buf.shape[1]), w_buf.dtype)

    @pl.when(gets)
    def _():
        edge.wait_recv()
        both = w_buf[0 : ROWS - FEW, :].astype(jnp.float32) + edge_buf[...].astype(jnp.float32)
        w_buf[0 : ROWS - FEW, :] = both.astype(w_buf.dtype)

    own_fill(1)

    for tick in range(COUNT + 9):

        def at(stage, act, direct=None):
            u = tick - stage
            if 0 <= u < COUNT and direct in (None, u in DIRECT):
                act(u)

        at(-1, own_send)
        at(1, lambda u: (bx_step(u), z_step(u, 1), far_step(u, 0)), False)
        at(1, lambda u: (bx_step(u), far_step(u, 0), z_step(u, 1), z_step(u, 2), z_step(u, 3)), True)
        at(3, lambda u: multiply(u, 0))
        at(2, lambda u: (row_step(u, 0), far_step(u, 1), z_step(u, 2)), False)
        at(2, lambda u: (row_step(u, 0), far_step(u, 1), far_step(u, 2), far_step(u, 3)), True)
        at(4, lambda u: multiply(u, 1))
        at(3, lambda u: (row_step(u, 1), far_step(u, 2), z_step(u, 3)), False)
        at(3, lambda u: (row_step(u, 1), row_step(u, 2), row_step(u, 3)), True)
        at(5, lambda u: multiply(u, 2), False)
        at(4, lambda u: (row_step(u, 2), far_step(u, 3)), False)
        at(5, lambda u: row_step(u, 3), False)
        at(6, lambda u: (multiply(u, 3), y_step(u)), False)
        at(4, lambda u: (multiply(u, 2), multiply(u, 3), y_step(u)), True)
        at(7, zs_step, False)
        at(5, zs_step, True)
        at(8, xs_step, False)
        at(6, xs_step, True)
        at(9, x_done, False)
        at(7, x_done, True)
        if tick == 1:
            v_copy.wait()
        if 1 <= tick <= NZ:
            turn_v((zz + (0, 1, 3, 2)[tick - 1]) % NZ)
        at(-2, own_fill)
        if tick == 0:
            def clear(step, carry):
                for t_buf in t_bufs:
                    t_buf[step // 8, step // 2 % 4, step % 2, ROWS:, :] = jnp.zeros((PAD - ROWS, t_buf.shape[-1]), jnp.bfloat16)

                @pl.when((step % 2 == kk) & jnp.logical_not((step // 8 == NZ - 1) & (kk == 1)))
                def _():
                    for t_buf in t_bufs[1:]:
                        t_buf[step // 8, step // 2 % 4, step % 2, FEW:ROWS, :] = jnp.zeros((ROWS - FEW, t_buf.shape[-1]), jnp.bfloat16)

                return carry

            lax.fori_loop(0, NX * NZ * NK, clear, 0)
            slot_pick()
        at(6, gather_sent, False)
        at(4, gather_sent, True)

    finish(UNITS[LAST][0])
    for u in range(COUNT):
        sent(r_bufs[u].at[0 : r_bufs[u].shape[0] // 4 * 3], kind(u, 5))
        sent(q_bufs[u].at[0 : NH * NZ - 1], kind(u, 6))


def local(tau, vvvv, scales, tile_ids, counts, spin_c, spin_d, pair_energy, ab_energy):
    slots, width, klayer = vvvv.shape
    pairs, kpiece = tau.shape
    ntile = lax.axis_size("tile")
    nlayer = lax.axis_size("layer")
    own_pairs = pairs // (nlayer * ntile)
    all_slots = slots * ntile
    vmem = pl.BlockSpec(memory_space=pltpu.VMEM)
    bf16, f32 = jnp.bfloat16, jnp.float32
    dma = pltpu.SemaphoreType.DMA
    columns = slots * width
    smem = pl.BlockSpec(memory_space=pltpu.SMEM)
    amplitudes = pl.pallas_call(
        ladder_kernel,
        out_shape=jax.ShapeDtypeStruct((all_slots, own_pairs, width), f32),
        in_specs=[vmem, pl.BlockSpec(memory_space=pl.ANY), smem, vmem, vmem, vmem, vmem, smem, vmem],
        out_specs=vmem,
        scratch_shapes=[
            pltpu.VMEM((own_pairs, NX * NK, NZ, columns), f32),
            pltpu.VMEM((slots, all_slots, ntile), f32),
            [pltpu.VMEM((NZ, NX, NK, PAD, lanes), bf16) for lanes in LANES],
            pltpu.VMEM((slots, klayer + 16, width), bf16),
            pltpu.VMEM((columns, ntile * PAD), bf16),
            pltpu.VMEM((ROWS, pairs), bf16),
            pltpu.VMEM((ROWS - FEW, pairs), bf16),
            [pltpu.VMEM((columns, lanes), f32) for lanes in LANES],
            [pltpu.VMEM((lanes, columns), f32) for lanes in LANES],
            [pltpu.VMEM((NY - 1, lanes // NY, columns), f32) for lanes in LANES],
            [pltpu.VMEM((NH * NZ, lanes // 32, columns), f32) for lanes in LANES],
            [pltpu.VMEM((NH * NZ, lanes // 32, columns), f32) for lanes in LANES],
            pltpu.VMEM((own_pairs, NX * NK, NZ, columns), f32),
            dma,
            dma((2,)),
            dma((COUNT, 10)),
            dma((COUNT, NZ)),
            dma((COUNT, NZ, 2)),
            dma((COUNT, 2)),
            dma((COUNT, NZ)),
            dma((COUNT, NZ)),
            dma((COUNT,)),
            dma((COUNT,)),
            dma((COUNT,)),
        ],
        compiler_params=pltpu.CompilerParams(
            collective_id=0, has_side_effects=True, vmem_limit_bytes=56 * 1024 * 1024
        ),
        name="ladder",
    )(tau.T, jnp.swapaxes(vvvv, 1, 2), scales, spin_c, spin_d, tile_ids, counts, pair_energy, ab_energy)
    return jnp.swapaxes(amplitudes, 0, 1).reshape(own_pairs, all_slots * width)


def solution(mesh):
    placed = (
        P(None, ("layer", "tile")),
        P("tile", None, "layer"),
        P("tile"),
        P(),
        P(),
        P(),
        P(),
        P(("layer", "tile")),
        P(),
    )
    return jax.shard_map(
        local, mesh=mesh, in_specs=placed, out_specs=P(("layer", "tile"), None), check_vma=False
    )
```

```python
import functools

import jax
import jax.numpy as jnp
from jax import lax
from jax.experimental import pallas as pl
from jax.experimental.pallas import tpu as pltpu
from jax.sharding import PartitionSpec as P

MESH = pl.DeviceIdType.MESH

NX, NZ, NK, NY, NH = 4, 4, 2, 4, 2
UNITS = ((0, (0, 1)), (1, (0, 1)), (2, (0, 1)), (3, (0,)), (3, (1,)))
LANES = tuple(128 * len(cores) for _, cores in UNITS)
COUNT = len(UNITS)
DIRECT = (4,)
LAST = COUNT - 1
ROWS = 240
FEW = 224
PAD = 256
A_ROWS = 176


def ladder_kernel(
    tau_ref,
    v_hbm,
    scales_ref,
    spin_c_ref,
    spin_d_ref,
    ids_ref,
    counts_ref,
    pair_ref,
    ab_ref,
    out_ref,
    own_buf,
    pick_buf,
    t_bufs,
    v_buf,
    vt_buf,
    w_buf,
    edge_buf,
    accs,
    r_bufs,
    y_bufs,
    q_bufs,
    z_bufs,
    s_buf,
    v_sem,
    edge_sem,
    send_sem,
    az_r,
    ax_r,
    bx_r,
    bz_r,
    sib_r,
    y_r,
    z_r,
    x_r,
):
    layer = lax.axis_index("layer")
    tile = lax.axis_index("tile")
    xx, zz, kk = tile // 8, (tile // 2) % 4, tile % 2
    hh, yy = layer // 4, layer % 4
    kpiece = tau_ref.shape[0]
    klayer = v_hbm.shape[1]
    virtual = spin_d_ref.shape[0]
    panel = spin_c_ref.shape[0]

    place = hh * NZ + zz

    def xdev(x, core=None):
        return (layer, x * 8 + zz * 2 + (kk if core is None else core))

    def zdev(z):
        return (layer, xx * 8 + z * 2 + kk)

    sib = xdev(xx, 1 - kk)

    def ydev(y):
        return (hh * 4 + y, tile)

    def ring(other):
        return (other // NZ * 4 + yy, xx * 8 + other % NZ * 2 + kk)

    barrier = pltpu.get_barrier_semaphore()

    def greet(dev):
        pl.semaphore_signal(barrier, inc=1, device_id=dev, device_id_type=MESH)

    for step in range(1, NH * NZ):
        greet(ring((place + step) % (NH * NZ)))
    for step in range(1, NY):
        greet(ydev((yy + step) % NY))
    for step in range(1, NX):
        greet(xdev((xx + step) % NX))
    for step in range(NX):
        greet(xdev((xx + step) % NX, 1 - kk))
    tiles = NX * NZ * NK
    greet((layer, (tile + 1) % tiles))
    greet((layer, (tile + tiles - 1) % tiles))

    v_copy = pltpu.make_async_copy(v_hbm, v_buf.at[:, pl.ds(0, klayer)], v_sem)
    v_copy.start()
    v_buf[:, klayer:, :] = jnp.zeros((v_buf.shape[0], v_buf.shape[1] - klayer, 128), v_buf.dtype)

    start = (kpiece * tile) // 16 * 16
    offset = kpiece * tile - start
    base = layer * klayer + start
    c_first = base // virtual
    d_first = base - c_first * virtual
    row = lax.broadcasted_iota(jnp.int32, (ROWS, 1), 0)
    d_index = row + d_first
    over = d_index >= virtual
    d_index = jnp.where(over, d_index - virtual, d_index)
    c_index = jnp.where(over, c_first + 1, c_first)
    d_iota = lax.broadcasted_iota(jnp.int32, (ROWS, virtual), 1)
    c_iota = lax.broadcasted_iota(jnp.int32, (ROWS, panel), 1)
    spin_right = jnp.sum(jnp.where(d_iota == d_index, spin_d_ref[...][None, :], 0).astype(jnp.float32), axis=1, keepdims=True)
    spin_left = jnp.sum(jnp.where(c_iota == c_index, spin_c_ref[...][None, :], 0).astype(jnp.float32), axis=1, keepdims=True)
    factor = jnp.where(spin_left == spin_right, 0.5, 1.0)
    shift = (
        lax.broadcasted_iota(jnp.int32, (ROWS, kpiece), 0) - offset
        == lax.broadcasted_iota(jnp.int32, (ROWS, kpiece), 1)
    )
    placed = jnp.dot(
        shift.astype(jnp.float32).astype(jnp.bfloat16), tau_ref[...], preferred_element_type=jnp.float32
    )
    w_buf[...] = (placed * factor).astype(jnp.bfloat16)

    part_a = pl.ds(0, A_ROWS)

    def b_rows(u, z0, act):
        if u == 0:
            act(pl.ds(A_ROWS, ROWS - A_ROWS))
            return
        wide = (z0 == NZ - 1) & (kk == 1)

        @pl.when(wide)
        def _():
            act(pl.ds(A_ROWS, ROWS - A_ROWS))

        @pl.when(jnp.logical_not(wide))
        def _():
            act(pl.ds(A_ROWS, FEW - A_ROWS))

    def copy(src, dst, ssem, rsem, dev):
        return pltpu.make_async_remote_copy(
            src_ref=src, dst_ref=dst, send_sem=ssem, recv_sem=rsem, device_id=dev, device_id_type=MESH
        )

    def same(ref, ssem, rsem, dev):
        return copy(ref, ref, ssem, rsem, dev)

    def kind(u, i):
        return send_sem.at[u, i]

    def az(u, z0, way):
        return same(t_bufs[u].at[z0, xx, kk, part_a], kind(u, 0 if way > 0 else 7), az_r.at[u, z0], zdev(zz + way))

    def bz(u, z0, way, rows):
        return same(t_bufs[u].at[z0, :, kk, rows], kind(u, 1 if way > 0 else 8), bz_r.at[u, z0], zdev(zz + way))

    def turn(u, z0):
        return 1 - 2 * ((u + z0) % 2)

    def ax(u, z0, way):
        s = turn(u, z0) if way == 2 else 1 - 2 * way
        source = (xx - s + 4) % 4 if way == 2 else xx
        return same(t_bufs[u].at[z0, source, kk, part_a], kind(u, 2), ax_r.at[u, z0, way // 2], xdev((xx + s + 4) % 4))

    def ax_near(u, z0):
        return same(t_bufs[u].at[z0, 0:2, kk, part_a], kind(u, 2), ax_r.at[u, z0, 0], sib)

    def ax_far(u, z0):
        return same(t_bufs[u].at[z0, (xx + 2) % 4, kk, part_a], kind(u, 2), ax_r.at[u, z0, 1], sib)

    def bx(u, way, rows):
        s = turn(u, 0) if way == 2 else 1 - 2 * way
        source = (xx - s + 4) % 4 if way == 2 else xx
        return same(t_bufs[u].at[zz, source, kk, rows], kind(u, 3), bx_r.at[u, way // 2], xdev((xx + s + 4) % 4))

    def bx_near(u, rows):
        return same(t_bufs[u].at[zz, 0:2, kk, rows], kind(u, 3), bx_r.at[u, 0], sib)

    def bx_far(u, rows):
        return same(t_bufs[u].at[zz, (xx + 2) % 4, kk, rows], kind(u, 3), bx_r.at[u, 1], sib)

    def sb(u, z0):
        return same(t_bufs[u].at[z0, :, kk, 0:ROWS], kind(u, 4), sib_r.at[u, z0], sib)

    def sides(distance, act):
        for sign in (-1, 1):
            z0 = zz + sign * distance

            @pl.when((z0 >= 0) & (z0 < NZ))
            def _():
                act(z0, sign)

    def pass_on(sign, send):
        if sign <= 0:

            @pl.when(zz < NZ - 1)
            def _():
                send(1)

        if sign >= 0:

            @pl.when(zz > 0)
            def _():
                send(-1)

    def rows_at(distance, act):
        act(zz, 0) if distance == 0 else sides(distance, act)

    def z_step(u, distance):
        def act(z0, sign):
            az(u, z0, 0).wait_recv()
            if u not in DIRECT:
                pass_on(sign, lambda way: az(u, z0, way).start())
            ax(u, z0, 0).start()
            ax(u, z0, 1).start()

        sides(distance, act)

    def far_step(u, distance):
        def act(z0, sign):
            ax_near(u, z0).wait_recv()
            ax(u, z0, 2).start()

        rows_at(distance, act)

    def row_step(u, distance):
        def act(z0, sign):
            def hop(rows):
                (bx_far(u, rows) if distance == 0 else bz(u, z0, 0, rows)).wait_recv()
                if u not in DIRECT:
                    pass_on(sign, lambda way: bz(u, z0, way, rows).start())
                elif distance == 0:
                    for d in (3, 2, 1):
                        sides(d, lambda _, side: bz(u, zz, side * d, rows).start())

            b_rows(u, z0, hop)
            ax_far(u, z0).wait_recv()
            sb(u, z0).start()

        rows_at(distance, act)

    def own_fill(u):
        j, cores = UNITS[u]
        n, lanes = len(cores), LANES[u]
        q = lax.broadcasted_iota(jnp.int32, (1, lanes), 1)
        q_y, q_h, q_z, q_k, q_x = q // (32 * n), q // (16 * n) % 2, q // (4 * n) % 4, q // 4 % n + cores[0], q % 4
        pair = (q_h * 4 + q_y) * 128 + (q_x * 8 + q_z * 2 + q_k) * 4 + j
        pick = lax.broadcasted_iota(jnp.int32, (tau_ref.shape[1], lanes), 0) == pair
        block = jnp.dot(
            w_buf[...], pick.astype(jnp.float32).astype(jnp.bfloat16), preferred_element_type=jnp.float32
        )
        t_bufs[u][zz, xx, kk, 0:ROWS, :] = block.astype(jnp.bfloat16)

    def own_send(u):
        if u in DIRECT:
            for d in (3, 2, 1):
                sides(d, lambda z0, sign: az(u, zz, sign * d).start())
        else:
            pass_on(0, lambda way: az(u, zz, way).start())
        b_rows(u, zz, lambda rows: (bx(u, 0, rows).start(), bx(u, 1, rows).start()))
        ax(u, zz, 0).start()
        ax(u, zz, 1).start()

    def bx_step(u):
        b_rows(u, zz, lambda rows: (bx_near(u, rows).wait_recv(), bx(u, 2, rows).start()))

    def turn_v(z0):
        def one(i, carry):
            t = i // NK * (NZ * NK) + z0 * NK + i % NK
            first = pl.multiple_of((kpiece * t) // 16 * 16, 16)
            lanes = pl.ds(pl.multiple_of((z0 * NX * NK + i) * PAD, PAD), PAD)
            for s in range(v_buf.shape[0]):
                vt_buf[s * 128 : (s + 1) * 128, lanes] = v_buf[s, pl.ds(first, PAD), :].T
            return carry

        lax.fori_loop(0, NX * NK, one, 0)

    def multiply(u, distance):
        depth = NX * NK * PAD

        def act(z0, sign):
            t_bufs_row = t_bufs[u].at[z0]
            same(t_bufs_row.at[:, 1 - kk, 0:ROWS], kind(u, 4), sib_r.at[u, z0], sib).wait_recv()
            if distance == 0:
                accs[u][...] = jnp.zeros(accs[u].shape, jnp.float32)

            def one(i, carry):
                size = depth // 2
                part = vt_buf[:, pl.ds(pl.multiple_of(z0 * depth + i * size, size), size)]
                block = t_bufs_row[pl.ds(i * 2, 2)].reshape(size, LANES[u])
                accs[u][...] += jnp.dot(part, block, preferred_element_type=jnp.float32)
                return carry

            lax.fori_loop(0, 2, one, 0)

        rows_at(distance, act)

    def y_step(u):
        r_buf = r_bufs[u]
        quarter = r_buf.shape[0] // NY
        for half in range(LANES[u] // 128):
            lanes = slice(half * 128, half * 128 + 128)
            for s in range(v_buf.shape[0]):
                rows = slice(s * 128, s * 128 + 128)
                r_buf[lanes, rows] = (accs[u][rows, lanes] * scales_ref[s]).T
        for step in (2, 1, 3):
            other = (yy + step) % NY
            rows = pl.ds(pl.multiple_of(other * quarter, quarter), quarter)
            copy(r_buf.at[rows], y_bufs[u].at[3 - step], kind(u, 5), y_r.at[u], ydev(other)).start()

    def finish(p):
        width = ab_ref.shape[1]
        owned = own_buf[p].reshape(NX * NK * NZ, own_buf.shape[3])
        residual = jnp.zeros(ab_ref.shape, jnp.float32)
        for s in range(v_buf.shape[0]):
            residual += jnp.dot(
                pick_buf[s],
                owned[:, s * width : (s + 1) * width],
                precision=lax.Precision.HIGHEST,
                preferred_element_type=jnp.float32,
            )
        out_ref[:, p, :] = residual / (ab_ref[...] - pair_ref[p])

    def x_done(u):
        j, cores = UNITS[u]
        for core in range(NK):
            if core in cores:

                @pl.when(kk == core)
                def _():
                    same(own_buf.at[j, 0 : NX * NK - 1], kind(u, 9), x_r.at[u], sib).wait_recv()

        if len(cores) == NK:
            sent(s_buf.at[j, 0 : NX * NK - 1], kind(u, 9))
            finish(j)
            return

        @pl.when(kk == cores[0])
        def _():
            sent(s_buf.at[j, 0 : NX - 1], kind(u, 9))

        @pl.when(kk != cores[0])
        def _():
            sent(s_buf.at[j, 0:NX], kind(u, 9))

        if u != LAST and all(place != j for place, _ in UNITS[u + 1 :]):
            finish(j)

    def zs_step(u):
        r_buf, y_buf, q_buf, z_buf = r_bufs[u], y_bufs[u], q_bufs[u], z_bufs[u]
        quarter = r_buf.shape[0] // NY
        rows = q_buf.shape[1]
        same(y_buf, kind(u, 5), y_r.at[u], sib).wait_recv()
        mine = r_buf[pl.ds(pl.multiple_of(yy * quarter, quarter), quarter), :]
        total = mine + y_buf[0] + y_buf[1] + y_buf[2]
        for other in range(NH * NZ):
            q_buf[other] = total[other * rows : (other + 1) * rows, :]
        z_buf[place] = q_buf[place]
        for step in (4, 3, 5, 2, 6, 1, 7):
            other = (place + step) % (NH * NZ)
            copy(q_buf.at[other], z_buf.at[place], kind(u, 6), z_r.at[u], ring(other)).start()

    def xs_step(u):
        z_buf = z_bufs[u]
        j, cores = UNITS[u]
        same(z_buf.at[0 : NH * NZ - 1], kind(u, 6), z_r.at[u], sib).wait_recv()
        for z in range(NZ):
            both = z_buf[z] + z_buf[NZ + z]
            for i, core in enumerate(cores):
                for x in range(NX):
                    s_buf[j, core * NX + x, z : z + 1, :] = both[i * NX + x : i * NX + x + 1, :]

        def send(core, step):
            other = (xx + step) % NX
            copy(s_buf.at[j, core * NX + other], own_buf.at[j, xx * NK + kk], kind(u, 9), x_r.at[u], xdev(other, core)).start()

        for core in cores:

            @pl.when(kk == core)
            def _():
                for step in (2, 1, 3):
                    send(core, step)
                own_buf[j, xx * NK + kk] = s_buf[j, core * NX + xx]

            @pl.when(kk != core)
            def _():
                for step in (2, 1, 3, 0):
                    send(core, step)

    def sent(ref, sem):
        same(ref, sem, sem, sib).wait_send()

    def gather_sent(u):
        t_buf = t_bufs[u]
        sent(t_buf.at[0:3, :, 0, part_a], kind(u, 2))
        b_rows(u, zz, lambda rows: sent(t_buf.at[0:3, 0, 0, rows], kind(u, 3)))
        sent(t_buf.at[:, :, 0, 0:ROWS], kind(u, 4))

        for v in range(NZ):

            @pl.when(zz == v)
            def _():
                if u in DIRECT:
                    for count, i in ((NZ - 1 - v, 0), (v, 7)):
                        if count:
                            sent(t_buf.at[0, 0:count, 0, part_a], kind(u, i))
                            b_rows(u, v, lambda rows: sent(t_buf.at[:, 0:count, 0, rows], kind(u, i + 1)))
                    return
                ups, downs = v + 1 if v < NZ - 1 else 0, NZ - v if v > 0 else 0
                few = pl.ds(A_ROWS, (ROWS if u == 0 else FEW) - A_ROWS)
                if ups:
                    sent(t_buf.at[0, 0:ups, 0, part_a], kind(u, 0))
                    sent(t_buf.at[:, 0:ups, 0, few], kind(u, 1))
                if downs:
                    sent(t_buf.at[0, 0:downs, 0, part_a], kind(u, 7))
                if downs and u == 0:
                    sent(t_buf.at[:, 0:downs, 0, few], kind(u, 8))
                elif downs:

                    @pl.when(kk == 1)
                    def _():
                        sent(t_buf.at[0, :, 0, 0 : (FEW - A_ROWS) * downs + ROWS - FEW], kind(u, 8))

                    @pl.when(kk != 1)
                    def _():
                        sent(t_buf.at[:, 0:downs, 0, few], kind(u, 8))

    def slot_pick():
        slots, owners = v_buf.shape[0], NX * NK * NZ
        g = lax.broadcasted_iota(jnp.int32, (owners, slots * owners), 1)
        t = lax.broadcasted_iota(jnp.int32, (owners, slots * owners), 0)
        held = jnp.where(g // slots == t, 1.0, 0.0).astype(jnp.bfloat16)
        counts = jnp.broadcast_to(counts_ref[...][None, :], (8, owners)).astype(jnp.float32).astype(jnp.bfloat16)
        count = jnp.dot(counts, held, preferred_element_type=jnp.float32)
        ids = jnp.broadcast_to(ids_ref[...][None, :], count.shape).astype(jnp.float32)
        slot = lax.broadcasted_iota(jnp.int32, count.shape, 1) % slots
        ids = jnp.where(slot.astype(jnp.float32) < count, ids, -1.0).astype(jnp.bfloat16)
        g = lax.broadcasted_iota(jnp.int32, (slots * owners, owners), 0)
        r = lax.broadcasted_iota(jnp.int32, (slots * owners, owners), 1)
        t = r // (NK * NZ) * (NK * NZ) + r % NZ * NK + r // NZ % NK
        j = lax.broadcasted_iota(jnp.int32, (slots * owners, owners), 0).astype(jnp.float32)
        for s in range(slots):
            order = jnp.where(g == t * slots + s, 1.0, 0.0).astype(jnp.bfloat16)
            mine = jnp.dot(ids, order, preferred_element_type=jnp.float32)
            pick_buf[s] = jnp.where(mine[0:1, :] == j, 1.0, 0.0)

    own_fill(0)
    pl.semaphore_wait(barrier, (NX - 1) + (NY - 1) + (NH * NZ - 1) + NX + 2)
    gives, gets = tile % 16 != 15, tile % 16 != 0
    edge = copy(w_buf.at[FEW:ROWS], edge_buf, edge_sem.at[0], edge_sem.at[1], (layer, (tile + 1) % tiles))

    @pl.when(gives)
    def _():
        edge.start()

    own_send(0)

    @pl.when(gives)
    def _():
        edge.wait_send()
        w_buf[FEW:ROWS, :] = jnp.zeros((ROWS - FEW, w_buf.shape[1]), w_buf.dtype)

    @pl.when(gets)
    def _():
        edge.wait_recv()
        both = w_buf[0 : ROWS - FEW, :].astype(jnp.float32) + edge_buf[...].astype(jnp.float32)
        w_buf[0 : ROWS - FEW, :] = both.astype(w_buf.dtype)

    own_fill(1)

    for tick in range(COUNT + 9):

        def at(stage, act, direct=None):
            u = tick - stage
            if 0 <= u < COUNT and direct in (None, u in DIRECT):
                act(u)

        at(-1, own_send)
        at(1, lambda u: (bx_step(u), z_step(u, 1), far_step(u, 0)), False)
        at(1, lambda u: (bx_step(u), far_step(u, 0), z_step(u, 1), z_step(u, 2), z_step(u, 3)), True)
        at(3, lambda u: multiply(u, 0))
        at(2, lambda u: (row_step(u, 0), far_step(u, 1), z_step(u, 2)), False)
        at(2, lambda u: (row_step(u, 0), far_step(u, 1), far_step(u, 2), far_step(u, 3)), True)
        at(4, lambda u: multiply(u, 1))
        at(3, lambda u: (row_step(u, 1), far_step(u, 2), z_step(u, 3)), False)
        at(3, lambda u: (row_step(u, 1), row_step(u, 2), row_step(u, 3)), True)
        at(5, lambda u: multiply(u, 2), False)
        at(4, lambda u: (row_step(u, 2), far_step(u, 3)), False)
        at(5, lambda u: row_step(u, 3), False)
        at(6, lambda u: (multiply(u, 3), y_step(u)), False)
        at(4, lambda u: (multiply(u, 2), multiply(u, 3), y_step(u)), True)
        at(7, zs_step, False)
        at(5, zs_step, True)
        at(8, xs_step, False)
        at(6, xs_step, True)
        at(9, x_done, False)
        at(7, x_done, True)
        if tick == COUNT + 6:
            for u in range(COUNT):
                sent(r_bufs[u].at[0 : r_bufs[u].shape[0] // 4 * 3], kind(u, 5))
                sent(q_bufs[u].at[0 : NH * NZ - 1], kind(u, 6))
        if tick == 1:
            v_copy.wait()
        if 1 <= tick <= NZ:
            turn_v((zz + (0, 1, 3, 2)[tick - 1]) % NZ)
        at(-2, own_fill)
        if tick == 0:
            def clear(step, carry):
                for t_buf in t_bufs:
                    t_buf[step // 8, step // 2 % 4, step % 2, ROWS:, :] = jnp.zeros((PAD - ROWS, t_buf.shape[-1]), jnp.bfloat16)

                @pl.when((step % 2 == kk) & jnp.logical_not((step // 8 == NZ - 1) & (kk == 1)))
                def _():
                    for t_buf in t_bufs[1:]:
                        t_buf[step // 8, step // 2 % 4, step % 2, FEW:ROWS, :] = jnp.zeros((ROWS - FEW, t_buf.shape[-1]), jnp.bfloat16)

                return carry

            lax.fori_loop(0, NX * NZ * NK, clear, 0)
            slot_pick()
        at(6, gather_sent, False)
        at(4, gather_sent, True)

    finish(UNITS[LAST][0])


def local(tau, vvvv, scales, tile_ids, counts, spin_c, spin_d, pair_energy, ab_energy):
    slots, width, klayer = vvvv.shape
    pairs, kpiece = tau.shape
    ntile = lax.axis_size("tile")
    nlayer = lax.axis_size("layer")
    own_pairs = pairs // (nlayer * ntile)
    all_slots = slots * ntile
    vmem = pl.BlockSpec(memory_space=pltpu.VMEM)
    bf16, f32 = jnp.bfloat16, jnp.float32
    dma = pltpu.SemaphoreType.DMA
    columns = slots * width
    smem = pl.BlockSpec(memory_space=pltpu.SMEM)
    amplitudes = pl.pallas_call(
        ladder_kernel,
        out_shape=jax.ShapeDtypeStruct((all_slots, own_pairs, width), f32),
        in_specs=[vmem, pl.BlockSpec(memory_space=pl.ANY), smem, vmem, vmem, vmem, vmem, smem, vmem],
        out_specs=vmem,
        scratch_shapes=[
            pltpu.VMEM((own_pairs, NX * NK, NZ, columns), f32),
            pltpu.VMEM((slots, all_slots, ntile), f32),
            [pltpu.VMEM((NZ, NX, NK, PAD, lanes), bf16) for lanes in LANES],
            pltpu.VMEM((slots, klayer + 16, width), bf16),
            pltpu.VMEM((columns, ntile * PAD), bf16),
            pltpu.VMEM((ROWS, pairs), bf16),
            pltpu.VMEM((ROWS - FEW, pairs), bf16),
            [pltpu.VMEM((columns, lanes), f32) for lanes in LANES],
            [pltpu.VMEM((lanes, columns), f32) for lanes in LANES],
            [pltpu.VMEM((NY - 1, lanes // NY, columns), f32) for lanes in LANES],
            [pltpu.VMEM((NH * NZ, lanes // 32, columns), f32) for lanes in LANES],
            [pltpu.VMEM((NH * NZ, lanes // 32, columns), f32) for lanes in LANES],
            pltpu.VMEM((own_pairs, NX * NK, NZ, columns), f32),
            dma,
            dma((2,)),
            dma((COUNT, 10)),
            dma((COUNT, NZ)),
            dma((COUNT, NZ, 2)),
            dma((COUNT, 2)),
            dma((COUNT, NZ)),
            dma((COUNT, NZ)),
            dma((COUNT,)),
            dma((COUNT,)),
            dma((COUNT,)),
        ],
        compiler_params=pltpu.CompilerParams(
            collective_id=0, has_side_effects=True, vmem_limit_bytes=56 * 1024 * 1024
        ),
        name="ladder",
    )(tau.T, jnp.swapaxes(vvvv, 1, 2), scales, spin_c, spin_d, tile_ids, counts, pair_energy, ab_energy)
    return jnp.swapaxes(amplitudes, 0, 1).reshape(own_pairs, all_slots * width)


def solution(mesh):
    placed = (
        P(None, ("layer", "tile")),
        P("tile", None, "layer"),
        P("tile"),
        P(),
        P(),
        P(),
        P(),
        P(("layer", "tile")),
        P(),
    )
    return jax.shard_map(
        local, mesh=mesh, in_specs=placed, out_specs=P(("layer", "tile"), None), check_vma=False
    )
```
